32 devices in a mesh: quad: 4 (over z), gy: 2 (over y), gx: 4 (over x, core).
Axes of the slice: x: 2, y: 2, z: 4, core: 2. Of those that a mesh axis runs over, the one named last changes fastest.
Arguments:
- modes_now: bfloat16 [1024, 16, 512], P('quad', 'gy', 'gx'), may hold values from -4 to 4
- basis_rows: bfloat16 [4096, 1024], P('quad'), may hold values from -0.25 to 0.25
- quad_weights: float32 [4096], P('quad'), may hold values from 0.2 to 2
- germ_nodes: float32 [4096, 8], P('quad'), may hold values from -1.5 to 1.5
- log_fields: float32 [8, 16, 512], P(None, 'gy', 'gx'), may hold values from -1 to 1
- reaction_rates: float32 [4096], P('quad'), may hold values from 0.08 to 0.32
Outputs:
- modes_next: float32 [1024, 16, 512], P('quad', 'gy', 'gx')
The draws below stay inside these ranges and needn't reach their ends.
All inputs are finite; a program needn't handle non-finite values.
Results may differ from the reference program's by a relative error of at most 0.02.
Values may be sent and summed in bfloat16 or wider, within the bound.
A program may use at most 64 MiB of HBM per device.

```python
import math
import jax
import jax.numpy as jnp
from jax import lax

MODES = 1024
QUAD_PTS = 4096
TERMS = 8
NY = 16
NX = 512
N_QUAD = 4


def strengthened(drawn, rng, source, target, parts, factor):
    owner, partner = [(jnp.arange(drawn.shape[dim]) // (drawn.shape[dim] // parts)).reshape([-1 if axis == dim else 1 for axis in range(drawn.ndim)]) for dim in (source, target)]
    chosen = jax.random.permutation(rng, parts)[partner]
    strong = (owner == chosen) | (owner == (partner + parts // 2) % parts)
    return jnp.where(strong, factor * drawn, drawn)


def levels(key, shape, shards, smallest, largest):
    def one(dim, parts):
        draws = jax.random.uniform(jax.random.fold_in(jax.random.fold_in(key, 6), dim), (parts,), jnp.float32, smallest / len(shards), largest / len(shards))
        return jnp.repeat(jnp.exp(draws), shape[dim] // parts).reshape((-1,) + (1,) * (len(shape) - dim - 1))

    loudness = one(*shards[0])
    for cut in shards[1:]:
        loudness = loudness * one(*cut)
    return loudness


def noise(key, shape, deviation, most, pieces=(), kind=jnp.bfloat16):
    entries = deviation * jax.random.normal(key, shape, jnp.float32)
    if pieces:
        entries = entries * levels(key, shape, pieces, -0.22, 0.18)
    return jnp.clip(entries, -most, most).astype(kind)


def noise_with(key, dims, width, bound, cuts, heavy, kind=jnp.bfloat16):
    entries = width * jax.random.normal(key, dims, jnp.float32)
    if cuts:
        entries = entries * levels(key, dims, cuts, -0.22, 0.18)
    return jnp.clip(strengthened(entries, jax.random.fold_in(key, 3), *heavy), -bound, bound).astype(kind)


def setup_inputs(seed: int = 0) -> dict:
    keys = jax.random.split(jax.random.key(seed), 7)
    return {
        "modes_now": noise(keys[0], (MODES, NY, NX), 1.0, 4.0, ((0, 4), (1, 2), (2, 4))),
        "basis_rows": noise_with(keys[1], (QUAD_PTS, MODES), MODES ** -0.5, 0.25, ((0, 4),), (0, 1, 4, 2.0)),
        "quad_weights": jnp.clip(jnp.exp(math.log(2.0) - 2.3025851 * jax.random.uniform(keys[2], (QUAD_PTS,), jnp.float32) ** levels(keys[2], (QUAD_PTS,), ((0, 4),), -0.2, 0.2)), 0.2, 2.0),
        "germ_nodes": jnp.clip(jax.random.uniform(keys[3], (QUAD_PTS, TERMS), jnp.float32, -1.5, 1.5) * levels(keys[3], (QUAD_PTS, TERMS), ((0, 4),), -0.4, 0.0), -1.5, 1.5),
        "log_fields": jnp.clip(jax.random.uniform(keys[4], (TERMS, NY, NX), jnp.float32, -1.0, 1.0) * levels(keys[4], (TERMS, NY, NX), ((1, 2), (2, 4)), -0.4, 0.0), -1.0, 1.0),
        "reaction_rates": jnp.clip(jnp.exp(math.log(0.32) - 1.3862944 * jax.random.uniform(keys[5], (QUAD_PTS,), jnp.float32) ** levels(keys[5], (QUAD_PTS,), ((0, 4),), -0.2, 0.2)), 0.08, 0.32),
    }


def neighbour(array, drow, dcol):
    return array[:, 1 + drow:array.shape[1] - 1 + drow, 1 + dcol:array.shape[2] - 1 + dcol]


def drive_of(field_ext, coeff_ext, rates, weights):
    center = neighbour(field_ext, 0, 0)
    coeff_mid = neighbour(coeff_ext, 0, 0)
    total = jnp.zeros_like(center)
    for drow, dcol in ((-1, 0), (1, 0), (0, -1), (0, 1)):
        total = total + (coeff_mid + neighbour(coeff_ext, drow, dcol)) * (neighbour(field_ext, drow, dcol) - center)
    total = total + rates[:, None, None] * (center - center * center * center)
    return (weights[:, None, None] * total).astype(jnp.bfloat16)


def project(iterate, basis_rows, quad_weights, germ_nodes, log_padded, reaction_rates):
    q_group = QUAD_PTS // N_QUAD
    flat = iterate.reshape(MODES, -1)

    def group(total, index):
        first = (index * q_group).astype(jnp.int32)
        rows = lax.dynamic_slice_in_dim(basis_rows, first, q_group, 0)
        nodes = lax.dynamic_slice_in_dim(germ_nodes, first, q_group, 0)
        weights = lax.dynamic_slice_in_dim(quad_weights, first, q_group, 0)
        rates = lax.dynamic_slice_in_dim(reaction_rates, first, q_group, 0)
        field = jnp.dot(rows, flat, preferred_element_type=jnp.float32).reshape(q_group, NY, NX)
        field_ext = jnp.pad(field, ((0, 0), (1, 1), (1, 1)))
        coeff_ext = jnp.exp(jnp.einsum("qj,jyx->qyx", nodes, log_padded, precision=lax.Precision.HIGHEST))
        weighted = drive_of(field_ext, coeff_ext, rates, weights).reshape(q_group, -1)
        part = lax.dot_general(rows, weighted, (((0,), (0,)), ((), ())), preferred_element_type=jnp.float32)
        rounded = lax.optimization_barrier(part.astype(jnp.bfloat16))
        return total + rounded.astype(jnp.float32), None

    start = jnp.zeros((MODES, NY * NX), jnp.float32)
    total, _ = lax.scan(group, start, jnp.arange(N_QUAD, dtype=jnp.int32))
    return total.reshape(MODES, NY, NX)


def reference(modes_now, basis_rows, quad_weights, germ_nodes, log_fields, reaction_rates):
    log_padded = jnp.pad(log_fields, ((0, 0), (1, 1), (1, 1)))
    first = project(modes_now, basis_rows, quad_weights, germ_nodes, log_padded, reaction_rates)
    iterate_one = (modes_now.astype(jnp.float32) + 0.04 * first).astype(jnp.bfloat16)
    second = project(iterate_one, basis_rows, quad_weights, germ_nodes, log_padded, reaction_rates)
    return modes_now.astype(jnp.float32) + 0.04 * second
```

```python
import functools

import jax
import jax.numpy as jnp
from jax import lax
from jax.experimental import pallas as pl
from jax.experimental.pallas import tpu as pltpu
from jax.sharding import PartitionSpec as P

time_step = 0.04
LANES = 128
GROUP = 16
NODE_PARTS = (0, 0, 1, 1, 0, 2)
LOG_PARTS = (0, 1, 0, 1, 2, 0)
MESH = pl.DeviceIdType.MESH


def split_parts(values, pattern):
    parts, rest = [], values
    for _ in range(3):
        part = rest.astype(jnp.bfloat16)
        parts.append(part.astype(jnp.float32))
        rest = rest - parts[-1]
    group = lax.broadcasted_iota(jnp.int32, values.shape, 1) // GROUP
    chosen = jnp.zeros_like(values)
    for index, which in enumerate(pattern):
        chosen = jnp.where(group == index, parts[which], chosen)
    return chosen.astype(jnp.bfloat16)


def spread(columns):
    padded = jnp.pad(columns, ((0, 0), (0, GROUP - columns.shape[1])))
    copies = len(NODE_PARTS)
    return jnp.pad(jnp.tile(padded, (1, copies)), ((0, 0), (0, LANES - copies * GROUP)))


def dot_nt(a, b):
    return lax.dot_general(a, b, (((1,), (1,)), ((), ())), preferred_element_type=jnp.float32)


def dot_nn(a, b):
    return jnp.dot(a, b, preferred_element_type=jnp.float32)


def picard_kernel(
    dims, modes_ref, basis_ref, aux_ref, logs_ref, out_ref,
    basis, first, second, halo_in, halo_out, field, coeff, weighted, outgoing, landed,
    local_sem, b_send, b_recv, m_send, m_recv, h_send, h_recv, o_send, o_recv,
):
    n, ny, nx, kl, ql, terms, rows, cols, qb = dims
    modes, cells, rim = n * kl, rows * cols, 2 * rows
    quad_pts, piece = n * ql, ql // (ny * nx)
    z, gy, gx = lax.axis_index("quad"), lax.axis_index("gy"), lax.axis_index("gx")
    even = lax.rem(gx, 2) == 0
    other_gy = 1 - gy
    other_core = gx + 1 - 2 * lax.rem(gx, 2)
    other_x = lax.rem(gx + 2, 4)
    to_x, to_y, to_core = (z, gy, other_x), (z, other_gy, gx), (z, gy, other_core)
    own = pl.ds(rim, cells)

    def block_of(rank):
        return jnp.where(even, rank, n - 1 - rank)

    def remote(src, dst, send, recv, target):
        return pltpu.make_async_remote_copy(
            src_ref=src, dst_ref=dst, send_sem=send, recv_sem=recv,
            device_id=target, device_id_type=MESH,
        )

    barrier = pltpu.get_barrier_semaphore()
    for step in range(1, n):
        pl.semaphore_signal(barrier, inc=1, device_id=(lax.rem(z + step, n), gy, gx), device_id_type=MESH)
    for step in range(1, nx):
        pl.semaphore_signal(barrier, inc=1, device_id=(z, gy, lax.rem(gx + step, nx)), device_id_type=MESH)
    pl.semaphore_signal(barrier, inc=1, device_id=to_y, device_id_type=MESH)
    pl.semaphore_wait(barrier, n + nx - 1)

    def modes_copy(rank):
        rows_of = pl.multiple_of(block_of(rank) * cells, cells)
        return modes_ref.at[pl.ds(rows_of, cells), :]

    def modes_slot(rank):
        return first.at[own, pl.ds(pl.multiple_of(rank * kl, kl), kl)]

    def peer(step):
        return lax.rem(z + step, n)

    load_basis = pltpu.make_async_copy(
        basis_ref, basis.at[pl.ds(pl.multiple_of(z * ql, ql), ql), pl.ds(0, modes)], local_sem.at[0]
    )
    load_basis.start()
    for step in range(1, n):
        remote(modes_copy(peer(step)), modes_slot(z), m_send.at[step], m_recv.at[step], (peer(step), gy, gx)).start()
    load_modes = pltpu.make_async_copy(modes_copy(z), modes_slot(z), local_sem.at[1])
    load_modes.start()
    basis[pl.ds(pl.multiple_of(z * ql, ql), ql), modes : modes + LANES] = split_parts(aux_ref[...], NODE_PARTS)
    load_basis.wait()

    def rows_at(shard, y, x, part=None):
        start = shard * ql + (y * nx + x) * piece
        if part is None:
            return basis.at[pl.ds(pl.multiple_of(start, piece), piece), :]
        half = piece // 2
        return basis.at[pl.ds(pl.multiple_of(start + part * half, half), half), :]

    Z, X, Y, DA, DB, S0, SX, SY, SA, SB, ZB = range(11)

    def push(ref, shard, kind, target, send_kind=None):
        send_kind = kind if send_kind is None else send_kind
        return remote(ref, ref, b_send.at[shard, send_kind], b_recv.at[shard, kind], target)

    def arrived(ref, shard, kind):
        push(ref, shard, kind, to_core).wait_recv()

    def up(shard):
        return push(rows_at(shard, gy, gx), shard, Z, (jnp.minimum(z + 1, n - 1), gy, gx))

    def down(shard):
        return push(rows_at(shard, gy, gx), shard, Z, (jnp.maximum(z - 1, 0), gy, gx), ZB)

    @pl.when(z < n - 1)
    def _():
        up(z).start()

    @pl.when(z > 0)
    def _():
        down(z).start()

    def plane(shard):
        mine = rows_at(shard, gy, gx)
        return [push(mine, shard, X, to_x), push(mine, shard, Y, to_y), push(mine, shard, S0, to_core)]

    def relay(shard):
        by_x, by_y = rows_at(shard, gy, other_x), rows_at(shard, other_gy, gx)
        return (
            [push(rows_at(shard, gy, other_x, 0), shard, DA, to_y), push(by_x, shard, SX, to_core)],
            [push(rows_at(shard, other_gy, gx, 1), shard, DB, to_x), push(by_y, shard, SY, to_core)],
        )

    def across(shard):
        return [
            push(rows_at(shard, other_gy, other_x, 0), shard, SA, to_core),
            push(rows_at(shard, other_gy, other_x, 1), shard, SB, to_core),
        ]

    def stage_z(shard):
        arrived(rows_at(shard, gy, gx), shard, Z)
        for copy in plane(shard):
            copy.start()

        @pl.when((shard < z) & (z < n - 1))
        def _():
            up(shard).start()

        @pl.when((shard > z) & (z > 0))
        def _():
            down(shard).start()

    def stage_xy(shard):
        after_x, after_y = relay(shard)
        arrived(rows_at(shard, gy, other_x), shard, X)
        for copy in after_x:
            copy.start()
        arrived(rows_at(shard, other_gy, gx), shard, Y)
        for copy in after_y:
            copy.start()

    def stage_d(shard):
        one, two = across(shard)
        arrived(rows_at(shard, other_gy, other_x, 0), shard, DA)
        one.start()
        arrived(rows_at(shard, other_gy, other_x, 1), shard, DB)
        two.start()

    def stage_s(shard):
        arrived(rows_at(shard, gy, other_core), shard, S0)
        core_x = lax.rem(other_core + 2, 4)
        arrived(rows_at(shard, gy, core_x), shard, SX)
        arrived(rows_at(shard, other_gy, other_core), shard, SY)
        arrived(rows_at(shard, other_gy, core_x, 0), shard, SA)
        arrived(rows_at(shard, other_gy, core_x, 1), shard, SB)

    def drain(shard):
        for copy in plane(shard) + relay(shard)[0] + relay(shard)[1] + across(shard):
            copy.wait_send()

        @pl.when((shard < z) & (z < n - 1))
        def _():
            up(shard).wait_send()

        @pl.when((shard > z) & (z > 0))
        def _():
            down(shard).wait_send()

    block = block_of(z)
    ahead = jnp.where(even, 1, -1)
    in_right, in_left = block < n - 1, block > 0
    has_right, has_left = in_right | (gx < nx - 1), in_left | (gx > 0)
    right_z, left_z = jnp.where(in_right, z + ahead, z), jnp.where(in_left, z - ahead, z)
    right_x = jnp.where(in_right, gx, jnp.minimum(gx + 1, nx - 1))
    left_x = jnp.where(in_left, gx, jnp.maximum(gx - 1, 0))

    def halo(turn, grid):
        width = grid.shape[1]
        span = pl.ds(0, width)
        hr, hs = h_recv, h_send
        lead, tail = grid.at[pl.ds(rim, rim), span], grid.at[pl.ds(cells, rim), span]
        before, after = grid.at[pl.ds(0, rim), span], grid.at[pl.ds(rim + cells, rim), span]
        top, bottom = halo_in.at[turn, pl.ds(0, cols), span], halo_in.at[turn, pl.ds(cols, cols), span]
        mine_last = halo_out.at[turn, pl.ds(0, cols), span]
        mine_lead = halo_out.at[turn, pl.ds(cols, cols), span]
        row = lax.broadcasted_iota(jnp.int32, (2 * cols, cells), 0)
        cell = lax.broadcasted_iota(jnp.int32, (2 * cols, cells), 1)
        wanted = jnp.where(row < cols, row * rows + rows - 1, (row - cols) * rows)
        pick = (wanted == cell).astype(jnp.float32).astype(jnp.bfloat16)

        steps = (
            (has_right, remote(tail, before, hs.at[turn, 0], hr.at[turn, 0], (right_z, gy, right_x)), has_left, before),
            (has_left, remote(lead, after, hs.at[turn, 1], hr.at[turn, 1], (left_z, gy, left_x)), has_right, after),
            (gy < ny - 1, remote(mine_last, top, hs.at[turn, 2], hr.at[turn, 2], to_y), gy > 0, top),
            (gy > 0, remote(mine_lead, bottom, hs.at[turn, 3], hr.at[turn, 3], to_y), gy < ny - 1, bottom),
        )

        def start():
            halo_out[turn, :, 0:width] = dot_nn(pick, grid[rim : rim + cells, :]).astype(jnp.bfloat16)
            for sends, copy, gets, slot in steps:

                @pl.when(sends)
                def _():
                    copy.start()

                @pl.when(jnp.logical_not(gets))
                def _():
                    slot[...] = jnp.zeros(slot.shape, jnp.bfloat16)

        def finish():
            for sends, copy, gets, slot in steps:

                @pl.when(gets)
                def _():
                    copy.wait_recv()

            cell_t = lax.broadcasted_iota(jnp.int32, (cells, 2 * cols), 0)
            row_t = lax.broadcasted_iota(jnp.int32, (cells, 2 * cols), 1)
            goal = jnp.where(row_t < cols, row_t * rows, (row_t - cols) * rows + rows - 1)
            place = (goal == cell_t).astype(jnp.float32).astype(jnp.bfloat16)
            grid[2 * rim + cells : 2 * rim + 2 * cells, :] = dot_nn(
                place, halo_in[turn, :, 0:width]
            ).astype(jnp.bfloat16)

        def drained():
            for sends, copy, gets, slot in steps:

                @pl.when(sends)
                def _():
                    copy.wait_send()

        return start, finish, drained

    lane = lax.broadcasted_iota(jnp.int32, (GROUP, LANES), 1)
    line = lax.broadcasted_iota(jnp.int32, (GROUP, LANES), 0)
    group = lane // GROUP
    whole = (group == 0) | (group == 2) | (group == 5)
    wants = (lane - group * GROUP) == terms + line
    select = jnp.where(whole & wants & (line < 2), 1.0, 0.0).astype(jnp.bfloat16)
    lanes = min(256, qb)
    slab = 2 * rows

    def drive(shard, grid):
        def step(i, _):
            start = pl.multiple_of(shard * ql + i * qb, qb)
            ext = basis[pl.ds(start, qb), modes : modes + LANES]
            field[...] = dot_nt(grid[:, 0:modes], basis[pl.ds(start, qb), 0:modes])
            coeff[...] = jnp.exp(dot_nt(first[:, modes : modes + LANES], ext))
            scalars = dot_nt(select, ext)
            y_at = lax.broadcasted_iota(jnp.int32, (2, rows, lanes), 1)
            for h in range(qb // lanes):
                part = slice(h * lanes, (h + 1) * lanes)
                weight, rate = scalars[0:1, part], scalars[1:2, part]
                for c in range(cells // slab):

                    def at(ref, offset):
                        return ref[offset + c * slab : offset + (c + 1) * slab, part]

                    mid, cm = at(field, rim), at(coeff, rim)
                    total = (cm + at(coeff, rim - rows)) * (at(field, rim - rows) - mid)
                    total += (cm + at(coeff, rim + rows)) * (at(field, rim + rows) - mid)
                    mid3, cm3 = mid.reshape(2, rows, lanes), cm.reshape(2, rows, lanes)
                    fh = at(field, 2 * rim + cells).reshape(2, rows, lanes)
                    ch = at(coeff, 2 * rim + cells).reshape(2, rows, lanes)
                    for shift, edge in ((1, 0), (rows - 1, rows - 1)):
                        fn = jnp.where(y_at == edge, fh, pltpu.roll(mid3, shift, 1))
                        cn = jnp.where(y_at == edge, ch, pltpu.roll(cm3, shift, 1))
                        total += ((cm3 + cn) * (fn - mid3)).reshape(slab, lanes)
                    total += rate * (mid - mid * mid * mid)
                    weighted[c * slab : (c + 1) * slab, pl.ds(start + h * lanes, lanes)] = (
                        weight * total
                    ).astype(jnp.bfloat16)
            return 0

        lax.fori_loop(0, ql // qb, step, 0)

    first[own, modes : modes + LANES] = split_parts(
        logs_ref[pl.ds(pl.multiple_of(block * cells, cells), cells), :], LOG_PARTS
    )
    load_modes.wait()
    for step in range(1, n):
        source = lax.rem(z - step + n, n)
        remote(modes_slot(source), modes_slot(source), m_send.at[step], m_recv.at[step], to_y).wait_recv()
    halo_a = halo(0, first)
    halo_a[0]()

    def nth(j):
        shard = jnp.int32(0)
        for rank in range(n):
            order = sorted((s for s in range(n) if s != rank), key=lambda s: (abs(s - rank), s))
            shard = shard + jnp.where(z == rank, order[j], 0)
        return shard

    shards = [nth(j) for j in range(n - 1)]
    stages = (stage_z, stage_xy, stage_d)
    stage_z(shards[0])
    halo_a[1]()
    drive(z, first)
    for turn in range(1, n + 1):
        for depth, stage in reversed(list(enumerate(stages))):
            j = turn - depth
            if 0 <= j < n - 1 and (j, depth) != (0, 0):
                stage(shards[j])
        j = turn - 2
        if 0 <= j < n - 1:
            stage_s(shards[j])
            drive(shards[j], first)

    def project(rank):
        span = pl.ds(pl.multiple_of(rank * kl, kl), kl)
        return span, dot_nn(weighted[...], basis[:, span])

    def update(rank, _):
        span, got = project(rank)
        now = first[own, span].astype(jnp.float32)
        second[own, span] = (now + time_step * got).astype(jnp.bfloat16)
        return 0

    lax.fori_loop(0, n, update, 0)

    halo_b = halo(1, second)
    halo_b[0]()
    halo_b[1]()
    lax.fori_loop(0, n, lambda shard, _: (drive(shard, second), 0)[1], 0)

    def landing(owner_block):
        return landed.at[pl.ds(pl.multiple_of(owner_block * cells, cells), cells), :]

    def deliver(step):
        return remote(
            outgoing.at[step], landing(block), o_send.at[step], o_recv.at[step], (peer(step), gy, gx)
        )

    for step in range(1, n):
        outgoing[step] = project(peer(step))[1].astype(jnp.bfloat16)
        deliver(step).start()
    landed[pl.ds(pl.multiple_of(block * cells, cells), cells), :] = project(z)[1].astype(jnp.bfloat16)
    for step in range(1, n):
        source = landing(block_of(lax.rem(z - step + n, n)))
        remote(source, source, o_send.at[step], o_recv.at[step], to_y).wait_recv()
    out_ref[...] = landed[...]

    for step in range(1, n):
        deliver(step).wait_send()
        remote(modes_copy(peer(step)), modes_slot(z), m_send.at[step], m_recv.at[step], (peer(step), gy, gx)).wait_send()
    halo_a[2]()
    halo_b[2]()

    @pl.when(z < n - 1)
    def _():
        up(z).wait_send()

    @pl.when(z > 0)
    def _():
        down(z).wait_send()

    for shard in shards:
        drain(shard)


def fast_body(n, ny, nx, modes_now, basis_rows, quad_weights, germ_nodes, log_fields, reaction_rates):
    kl, rows, width = modes_now.shape
    ql, modes = basis_rows.shape
    terms = germ_nodes.shape[1]
    cols = width // n
    cells, tile, rim, quad_pts = rows * cols, rows * width, 2 * rows, n * ql
    qb = min(512, ql)
    ext = modes + LANES
    dims = (n, ny, nx, kl, ql, terms, rows, cols, qb)
    modes_t = modes_now.transpose(2, 1, 0).reshape(tile, kl)
    aux = spread(jnp.concatenate([germ_nodes, quad_weights[:, None], reaction_rates[:, None]], axis=1))
    logs = spread(log_fields.transpose(2, 1, 0).reshape(tile, terms))
    any_spec, vmem = pl.BlockSpec(memory_space=pl.ANY), pl.BlockSpec(memory_space=pltpu.VMEM)
    grid_rows = 2 * rim + 2 * cells
    bf16, f32 = jnp.bfloat16, jnp.float32
    dma = pltpu.SemaphoreType.DMA
    delta_t = pl.pallas_call(
        functools.partial(picard_kernel, dims),
        out_shape=jax.ShapeDtypeStruct((tile, kl), bf16),
        in_specs=[any_spec, any_spec, vmem, vmem],
        out_specs=vmem,
        scratch_shapes=[
            pltpu.VMEM((quad_pts, ext), bf16),
            pltpu.VMEM((grid_rows, ext), bf16),
            pltpu.VMEM((grid_rows, modes), bf16),
            pltpu.VMEM((2, 2 * cols, ext), bf16),
            pltpu.VMEM((2, 2 * cols, ext), bf16),
            pltpu.VMEM((grid_rows, qb), f32),
            pltpu.VMEM((grid_rows, qb), f32),
            pltpu.VMEM((cells, quad_pts), bf16),
            pltpu.VMEM((n, cells, kl), bf16),
            pltpu.VMEM((tile, kl), bf16),
            dma((2,)),
            dma((n, 11)),
            dma((n, 11)),
            dma((n,)),
            dma((n,)),
            dma((2, 4)),
            dma((2, 4)),
            dma((n,)),
            dma((n,)),
        ],
        compiler_params=pltpu.CompilerParams(
            collective_id=0, has_side_effects=True, vmem_limit_bytes=48 * 1024 * 1024
        ),
    )(modes_t, basis_rows, aux, logs)
    delta = delta_t.reshape(width, rows, kl).transpose(2, 1, 0)
    return modes_now.astype(f32) + time_step * delta.astype(f32)


def with_halo(array, sides, width):
    for axis, dim in sides:
        peers, length = (lax.axis_size(axis), array.shape[dim])
        up = [(i, (i + 1) % peers) for i in range(peers - 1)]
        down = [(j, i) for i, j in up]
        last = lax.slice_in_dim(array, length - width, length, axis=dim)
        leading = lax.slice_in_dim(array, 0, width, axis=dim)
        before = lax.ppermute(last, axis, up)
        after = lax.ppermute(leading, axis, down)
        array = jnp.concatenate([before, array, after], axis=dim)
    return array


def neighbour(array, drow, dcol):
    return array[:, 1 + drow : array.shape[1] - 1 + drow, 1 + dcol : array.shape[2] - 1 + dcol]


def drive_with(field_ext, coeff_ext, rates, weights):
    center = neighbour(field_ext, 0, 0)
    coeff_mid = neighbour(coeff_ext, 0, 0)
    total = jnp.zeros_like(center)
    for drow, dcol in ((-1, 0), (1, 0), (0, -1), (0, 1)):
        total = total + (coeff_mid + neighbour(coeff_ext, drow, dcol)) * (
            neighbour(field_ext, drow, dcol) - center
        )
    total = total + rates[:, None, None] * (center - center * center * center)
    return (weights[:, None, None] * total).astype(jnp.bfloat16).reshape(center.shape[0], -1)


def rim_fields(field):
    return with_halo(field, (("gy", 1), ("gx", 2)), 1)


def body(modes_now, basis_rows, quad_weights, germ_nodes, log_fields, reaction_rates):
    k_local, rows_y, cols_x = modes_now.shape
    q_local, modes_total = basis_rows.shape
    log_ext = with_halo(log_fields, (("gy", 1), ("gx", 2)), 1)
    coeff_ext = jnp.exp(
        jnp.einsum("qj,jyx->qyx", germ_nodes, log_ext, precision=lax.Precision.HIGHEST)
    )

    def drive(field_ext):
        return drive_with(field_ext, coeff_ext, reaction_rates, quad_weights)

    current = modes_now.astype(jnp.float32)
    gathered = lax.all_gather(modes_now.reshape(k_local, -1), "quad", axis=0, tiled=True)
    field_zero = jnp.dot(basis_rows, gathered, preferred_element_type=jnp.float32)
    field_zero = rim_fields(field_zero.reshape(q_local, rows_y, cols_x))
    inner = gathered.reshape(modes_total, rows_y, cols_x)
    weighted_zero = drive(field_zero)
    partial_sum = lax.dot_general(
        basis_rows, weighted_zero, (((0,), (0,)), ((), ())), preferred_element_type=jnp.float32
    )
    summed = (
        lax.psum(partial_sum.astype(jnp.bfloat16), "quad")
        .astype(jnp.float32)
        .reshape(modes_total, rows_y, cols_x)
    )
    iterate_one = (inner.astype(jnp.float32) + time_step * summed).astype(jnp.bfloat16)
    flat = iterate_one.reshape(modes_total, -1)
    field_one = rim_fields(
        jnp.dot(basis_rows, flat, preferred_element_type=jnp.float32).reshape(
            q_local, rows_y, cols_x
        )
    )
    weighted = drive(field_one)
    second = (
        lax.psum_scatter(
            lax.dot_general(
                basis_rows, weighted, (((0,), (0,)), ((), ())), preferred_element_type=jnp.float32
            ).astype(jnp.bfloat16),
            "quad",
            scatter_dimension=0,
            tiled=True,
        )
        .astype(jnp.float32)
        .reshape(k_local, rows_y, cols_x)
    )
    return current + time_step * second


def solution(mesh):
    n, ny, nx = (mesh.shape[name] for name in ("quad", "gy", "gx"))
    planar = (ny, nx) == (2, 4) and n > 1
    run = functools.partial(fast_body, n, ny, nx) if planar else body
    in_specs = (
        P("quad", "gy", "gx"),
        P("quad", None),
        P("quad"),
        P("quad", None),
        P(None, "gy", "gx"),
        P("quad"),
    )
    out_specs = P("quad", "gy", "gx")
    return jax.shard_map(run, mesh=mesh, in_specs=in_specs, out_specs=out_specs, check_vma=False)
```

```python
import functools

import jax
import jax.numpy as jnp
from jax import lax
from jax.experimental import pallas as pl
from jax.experimental.pallas import tpu as pltpu
from jax.sharding import PartitionSpec as P

time_step = 0.04
LANES = 128
GROUP = 16
NODE_PARTS = (0, 0, 1, 1, 0, 2)
LOG_PARTS = (0, 1, 0, 1, 2, 0)
MESH = pl.DeviceIdType.MESH


def split_parts(values, pattern):
    parts, rest = [], values
    for _ in range(3):
        part = rest.astype(jnp.bfloat16)
        parts.append(part.astype(jnp.float32))
        rest = rest - parts[-1]
    group = lax.broadcasted_iota(jnp.int32, values.shape, 1) // GROUP
    chosen = jnp.zeros_like(values)
    for index, which in enumerate(pattern):
        chosen = jnp.where(group == index, parts[which], chosen)
    return chosen.astype(jnp.bfloat16)


def spread(columns):
    padded = jnp.pad(columns, ((0, 0), (0, GROUP - columns.shape[1])))
    copies = len(NODE_PARTS)
    return jnp.pad(jnp.tile(padded, (1, copies)), ((0, 0), (0, LANES - copies * GROUP)))


def dot_nt(a, b):
    return lax.dot_general(a, b, (((1,), (1,)), ((), ())), preferred_element_type=jnp.float32)


def dot_nn(a, b):
    return jnp.dot(a, b, preferred_element_type=jnp.float32)


def picard_kernel(
    dims, modes_ref, basis_ref, aux_ref, logs_ref, out_ref,
    basis, first, second, halo_out, field_a, field_b, coeff, faces, weighted, outgoing, landed,
    local_sem, b_send, b_recv, m_send, m_recv, h_send, h_recv, o_send, o_recv,
):
    n, ny, nx, kl, ql, terms, rows, cols, qb = dims
    modes, cells, rim = n * kl, rows * cols, 2 * rows
    quad_pts, piece = n * ql, ql // (ny * nx)
    z, gy, gx = lax.axis_index("quad"), lax.axis_index("gy"), lax.axis_index("gx")
    even = lax.rem(gx, 2) == 0
    other_gy = 1 - gy
    other_core = gx + 1 - 2 * lax.rem(gx, 2)
    other_x = lax.rem(gx + 2, 4)
    to_x, to_y, to_core = (z, gy, other_x), (z, other_gy, gx), (z, gy, other_core)
    own, edge = pl.ds(rim, cells), 2 * rim + cells

    def block_of(rank):
        return jnp.where(even, rank, n - 1 - rank)

    def remote(src, dst, send, recv, target):
        return pltpu.make_async_remote_copy(
            src_ref=src, dst_ref=dst, send_sem=send, recv_sem=recv,
            device_id=target, device_id_type=MESH,
        )

    barrier = pltpu.get_barrier_semaphore()
    for step in range(1, n):
        pl.semaphore_signal(barrier, inc=1, device_id=(lax.rem(z + step, n), gy, gx), device_id_type=MESH)
    for step in range(1, nx):
        pl.semaphore_signal(barrier, inc=1, device_id=(z, gy, lax.rem(gx + step, nx)), device_id_type=MESH)
    pl.semaphore_signal(barrier, inc=1, device_id=to_y, device_id_type=MESH)
    pl.semaphore_wait(barrier, n + nx - 1)

    def modes_copy(rank):
        rows_of = pl.multiple_of(block_of(rank) * cells, cells)
        return modes_ref.at[pl.ds(rows_of, cells), :]

    def modes_slot(rank):
        return first.at[own, pl.ds(pl.multiple_of(rank * kl, kl), kl)]

    def peer(step):
        return lax.rem(z + step, n)

    load_basis = pltpu.make_async_copy(
        basis_ref, basis.at[pl.ds(pl.multiple_of(z * ql, ql), ql), pl.ds(0, modes)], local_sem.at[0]
    )
    load_basis.start()
    for step in range(1, n):
        remote(modes_copy(peer(step)), modes_slot(z), m_send.at[step], m_recv.at[step], (peer(step), gy, gx)).start()
    load_modes = pltpu.make_async_copy(modes_copy(z), modes_slot(z), local_sem.at[1])
    load_modes.start()
    basis[pl.ds(pl.multiple_of(z * ql, ql), ql), modes : modes + LANES] = split_parts(aux_ref[...], NODE_PARTS)
    load_basis.wait()

    def rows_at(shard, y, x, part=None):
        start = shard * ql + (y * nx + x) * piece
        if part is None:
            return basis.at[pl.ds(pl.multiple_of(start, piece), piece), :]
        half = piece // 2
        return basis.at[pl.ds(pl.multiple_of(start + part * half, half), half), :]

    Z, X, Y, DA, DB, S0, SX, SY, SA, SB, ZB = range(11)

    def push(ref, shard, kind, target, send_kind=None):
        send_kind = kind if send_kind is None else send_kind
        return remote(ref, ref, b_send.at[shard, send_kind], b_recv.at[shard, kind], target)

    def arrived(ref, shard, kind):
        push(ref, shard, kind, to_core).wait_recv()

    def up(shard):
        return push(rows_at(shard, gy, gx), shard, Z, (jnp.minimum(z + 1, n - 1), gy, gx))

    def down(shard):
        return push(rows_at(shard, gy, gx), shard, Z, (jnp.maximum(z - 1, 0), gy, gx), ZB)

    @pl.when(z < n - 1)
    def _():
        up(z).start()

    @pl.when(z > 0)
    def _():
        down(z).start()

    def plane(shard):
        mine = rows_at(shard, gy, gx)
        return [push(mine, shard, X, to_x), push(mine, shard, Y, to_y), push(mine, shard, S0, to_core)]

    def relay(shard):
        by_x, by_y = rows_at(shard, gy, other_x), rows_at(shard, other_gy, gx)
        return (
            [push(rows_at(shard, gy, other_x, 0), shard, DA, to_y), push(by_x, shard, SX, to_core)],
            [push(rows_at(shard, other_gy, gx, 1), shard, DB, to_x), push(by_y, shard, SY, to_core)],
        )

    def across(shard):
        return [
            push(rows_at(shard, other_gy, other_x, 0), shard, SA, to_core),
            push(rows_at(shard, other_gy, other_x, 1), shard, SB, to_core),
        ]

    def stage_z(shard):
        arrived(rows_at(shard, gy, gx), shard, Z)
        for copy in plane(shard):
            copy.start()

        @pl.when((shard < z) & (z < n - 1))
        def _():
            up(shard).start()

        @pl.when((shard > z) & (z > 0))
        def _():
            down(shard).start()

    def stage_xy(shard):
        after_x, after_y = relay(shard)
        arrived(rows_at(shard, gy, other_x), shard, X)
        for copy in after_x:
            copy.start()
        arrived(rows_at(shard, other_gy, gx), shard, Y)
        for copy in after_y:
            copy.start()

    def stage_d(shard):
        one, two = across(shard)
        arrived(rows_at(shard, other_gy, other_x, 0), shard, DA)
        one.start()
        arrived(rows_at(shard, other_gy, other_x, 1), shard, DB)
        two.start()

    def stage_s(shard):
        arrived(rows_at(shard, gy, other_core), shard, S0)
        core_x = lax.rem(other_core + 2, 4)
        arrived(rows_at(shard, gy, core_x), shard, SX)
        arrived(rows_at(shard, other_gy, other_core), shard, SY)
        arrived(rows_at(shard, other_gy, core_x, 0), shard, SA)
        arrived(rows_at(shard, other_gy, core_x, 1), shard, SB)

    def drain(shard):
        for copy in plane(shard) + relay(shard)[0] + relay(shard)[1] + across(shard):
            copy.wait_send()

        @pl.when((shard < z) & (z < n - 1))
        def _():
            up(shard).wait_send()

        @pl.when((shard > z) & (z > 0))
        def _():
            down(shard).wait_send()

    block = block_of(z)
    ahead = jnp.where(even, 1, -1)
    in_right, in_left = block < n - 1, block > 0
    has_right, has_left = in_right | (gx < nx - 1), in_left | (gx > 0)
    right_z, left_z = jnp.where(in_right, z + ahead, z), jnp.where(in_left, z - ahead, z)
    right_x = jnp.where(in_right, gx, jnp.minimum(gx + 1, nx - 1))
    left_x = jnp.where(in_left, gx, jnp.maximum(gx - 1, 0))

    def halo(turn, grid):
        width = grid.shape[1]
        span = pl.ds(0, width)
        hr, hs = h_recv, h_send
        lead, tail = grid.at[pl.ds(rim, rim), span], grid.at[pl.ds(cells, rim), span]
        before, after = grid.at[pl.ds(0, rim), span], grid.at[pl.ds(rim + cells, rim), span]
        top, bottom = grid.at[pl.ds(edge, cols), span], grid.at[pl.ds(edge + cols, cols), span]
        mine_last = halo_out.at[turn, pl.ds(0, cols), span]
        mine_lead = halo_out.at[turn, pl.ds(cols, cols), span]
        row = lax.broadcasted_iota(jnp.int32, (2 * cols, cells), 0)
        cell = lax.broadcasted_iota(jnp.int32, (2 * cols, cells), 1)
        wanted = jnp.where(row < cols, row * rows + rows - 1, (row - cols) * rows)
        pick = (wanted == cell).astype(jnp.float32).astype(jnp.bfloat16)

        steps = (
            (has_right, remote(tail, before, hs.at[turn, 0], hr.at[turn, 0], (right_z, gy, right_x)), has_left, before),
            (has_left, remote(lead, after, hs.at[turn, 1], hr.at[turn, 1], (left_z, gy, left_x)), has_right, after),
            (gy < ny - 1, remote(mine_last, top, hs.at[turn, 2], hr.at[turn, 2], to_y), gy > 0, top),
            (gy > 0, remote(mine_lead, bottom, hs.at[turn, 3], hr.at[turn, 3], to_y), gy < ny - 1, bottom),
        )

        def start():
            halo_out[turn, :, 0:width] = dot_nn(pick, grid[rim : rim + cells, :]).astype(jnp.bfloat16)
            for sends, copy, gets, slot in steps:

                @pl.when(sends)
                def _():
                    copy.start()

                @pl.when(jnp.logical_not(gets))
                def _():
                    slot[...] = jnp.zeros(slot.shape, jnp.bfloat16)

        def finish():
            for sends, copy, gets, slot in steps:

                @pl.when(gets)
                def _():
                    copy.wait_recv()

        def drained():
            for sends, copy, gets, slot in steps:

                @pl.when(sends)
                def _():
                    copy.wait_send()

        return start, finish, drained

    lane = lax.broadcasted_iota(jnp.int32, (GROUP, LANES), 1)
    line = lax.broadcasted_iota(jnp.int32, (GROUP, LANES), 0)
    group = lane // GROUP
    whole = (group == 0) | (group == 2) | (group == 5)
    wants = (lane - group * GROUP) == terms + line
    select = jnp.where(whole & wants & (line < 2), 1.0, 0.0).astype(jnp.bfloat16)
    lanes = min(256, qb)
    slab = 2 * rows

    def start_of(block_index):
        return pl.multiple_of(block_index * qb, qb)

    def multiply(field, block_index, grid):
        field[...] = dot_nt(grid[:, 0:modes], basis[pl.ds(start_of(block_index), qb), 0:modes])

    def drive(field, block_index, fresh):
        start = start_of(block_index)
        ext = basis[pl.ds(start, qb), modes : modes + LANES]
        scalars = dot_nt(select, ext)
        if fresh:
            coeff[...] = jnp.exp(dot_nt(first[:, modes : modes + LANES], ext))
        y_at = lax.broadcasted_iota(jnp.int32, (rows, lanes), 0)
        for h in range(qb // lanes):
            part = slice(h * lanes, (h + 1) * lanes)
            here = pl.ds(start + h * lanes, lanes)
            weight, rate = scalars[0:1, part], scalars[1:2, part]

            def sides(ref, column):
                low = rim + column * rows
                mid = ref[low : low + rows, part]
                above = ref[edge + column : edge + column + 1, part]
                below = ref[edge + cols + column : edge + cols + column + 1, part]
                return mid, (
                    ref[low - rows : low, part],
                    ref[low + rows : low + 2 * rows, part],
                    jnp.where(y_at == 0, above, pltpu.roll(mid, 1, 0)),
                    jnp.where(y_at == rows - 1, below, pltpu.roll(mid, rows - 1, 0)),
                )

            for c in range(cols // 2):
                results = []
                for column in (2 * c, 2 * c + 1):
                    at = slice(column * rows, (column + 1) * rows)
                    mid, around = sides(field, column)
                    if fresh:
                        cm, others = sides(coeff, column)
                        sums = [cm + other for other in others]
                        for side, value in enumerate(sums):
                            faces[side, at, here] = value
                    else:
                        sums = [faces[side, at, here] for side in range(4)]
                    total = rate * (mid - mid * mid * mid)
                    for value, other in zip(sums, around):
                        total += value * (other - mid)
                    results.append(weight * total)
                weighted[c * slab : (c + 1) * slab, here] = jnp.concatenate(results, axis=0).astype(
                    jnp.bfloat16
                )

    per_shard = ql // qb
    fields = (field_a, field_b)

    def drive_shard(shard):
        base = shard * per_shard
        multiply(fields[0], base, first)
        for i in range(per_shard):
            if i + 1 < per_shard:
                multiply(fields[(i + 1) % 2], base + i + 1, first)
            drive(fields[i % 2], base + i, True)

    def drive_all():
        count = n * per_shard

        def pair(i, _):
            multiply(field_b, 2 * i + 1, second)
            drive(field_a, 2 * i, False)
            multiply(field_a, jnp.minimum(2 * i + 2, count - 1), second)
            drive(field_b, 2 * i + 1, False)
            return 0

        multiply(field_a, 0, second)
        lax.fori_loop(0, count // 2, pair, 0)

    first[own, modes : modes + LANES] = split_parts(
        logs_ref[pl.ds(pl.multiple_of(block * cells, cells), cells), :], LOG_PARTS
    )
    load_modes.wait()
    for step in range(1, n):
        source = lax.rem(z - step + n, n)
        remote(modes_slot(source), modes_slot(source), m_send.at[step], m_recv.at[step], to_y).wait_recv()
    halo_a = halo(0, first)
    halo_a[0]()

    def nth(j):
        shard = jnp.int32(0)
        for rank in range(n):
            order = sorted((s for s in range(n) if s != rank), key=lambda s: (abs(s - rank), s))
            shard = shard + jnp.where(z == rank, order[j], 0)
        return shard

    shards = [nth(j) for j in range(n - 1)]
    stages = (stage_z, stage_xy, stage_d)
    stage_z(shards[0])
    halo_a[1]()
    drive_shard(z)
    for turn in range(1, n + 1):
        for depth, stage in reversed(list(enumerate(stages))):
            j = turn - depth
            if 0 <= j < n - 1 and (j, depth) != (0, 0):
                stage(shards[j])
        j = turn - 2
        if 0 <= j < n - 1:
            stage_s(shards[j])
            drive_shard(shards[j])

    def project(rank):
        span = pl.ds(pl.multiple_of(rank * kl, kl), kl)
        return span, dot_nn(weighted[...], basis[:, span])

    def update(rank, _):
        span, got = project(rank)
        now = first[own, span].astype(jnp.float32)
        second[own, span] = (now + time_step * got).astype(jnp.bfloat16)
        return 0

    lax.fori_loop(0, n, update, 0)

    halo_b = halo(1, second)
    halo_b[0]()
    halo_b[1]()
    drive_all()

    def landing(owner_block):
        return landed.at[pl.ds(pl.multiple_of(owner_block * cells, cells), cells), :]

    def deliver(step):
        return remote(
            outgoing.at[step], landing(block), o_send.at[step], o_recv.at[step], (peer(step), gy, gx)
        )

    for step in range(1, n):
        outgoing[step] = project(peer(step))[1].astype(jnp.bfloat16)
        deliver(step).start()
    landed[pl.ds(pl.multiple_of(block * cells, cells), cells), :] = project(z)[1].astype(jnp.bfloat16)
    for step in range(1, n):
        source = landing(block_of(lax.rem(z - step + n, n)))
        remote(source, source, o_send.at[step], o_recv.at[step], to_y).wait_recv()
    out_ref[...] = landed[...]

    for step in range(1, n):
        deliver(step).wait_send()
        remote(modes_copy(peer(step)), modes_slot(z), m_send.at[step], m_recv.at[step], (peer(step), gy, gx)).wait_send()
    halo_a[2]()
    halo_b[2]()

    @pl.when(z < n - 1)
    def _():
        up(z).wait_send()

    @pl.when(z > 0)
    def _():
        down(z).wait_send()

    for shard in shards:
        drain(shard)


def fast_body(n, ny, nx, modes_now, basis_rows, quad_weights, germ_nodes, log_fields, reaction_rates):
    kl, rows, width = modes_now.shape
    ql, modes = basis_rows.shape
    terms = germ_nodes.shape[1]
    cols = width // n
    cells, tile, rim, quad_pts = rows * cols, rows * width, 2 * rows, n * ql
    qb = min(512, ql)
    ext = modes + LANES
    dims = (n, ny, nx, kl, ql, terms, rows, cols, qb)
    modes_t = modes_now.transpose(2, 1, 0).reshape(tile, kl)
    aux = spread(jnp.concatenate([germ_nodes, quad_weights[:, None], reaction_rates[:, None]], axis=1))
    logs = spread(log_fields.transpose(2, 1, 0).reshape(tile, terms))
    any_spec, vmem = pl.BlockSpec(memory_space=pl.ANY), pl.BlockSpec(memory_space=pltpu.VMEM)
    grid_rows = 2 * rim + cells + 2 * cols
    bf16, f32 = jnp.bfloat16, jnp.float32
    dma = pltpu.SemaphoreType.DMA
    delta_t = pl.pallas_call(
        functools.partial(picard_kernel, dims),
        out_shape=jax.ShapeDtypeStruct((tile, kl), bf16),
        in_specs=[any_spec, any_spec, vmem, vmem],
        out_specs=vmem,
        scratch_shapes=[
            pltpu.VMEM((quad_pts, ext), bf16),
            pltpu.VMEM((grid_rows, ext), bf16),
            pltpu.VMEM((grid_rows, modes), bf16),
            pltpu.VMEM((2, 2 * cols, ext), bf16),
            pltpu.VMEM((grid_rows, qb), f32),
            pltpu.VMEM((grid_rows, qb), f32),
            pltpu.VMEM((grid_rows, qb), f32),
            pltpu.VMEM((4, cells, quad_pts), f32),
            pltpu.VMEM((cells, quad_pts), bf16),
            pltpu.VMEM((n, cells, kl), bf16),
            pltpu.VMEM((tile, kl), bf16),
            dma((2,)),
            dma((n, 11)),
            dma((n, 11)),
            dma((n,)),
            dma((n,)),
            dma((2, 4)),
            dma((2, 4)),
            dma((n,)),
            dma((n,)),
        ],
        compiler_params=pltpu.CompilerParams(
            collective_id=0, has_side_effects=True, vmem_limit_bytes=48 * 1024 * 1024
        ),
    )(modes_t, basis_rows, aux, logs)
    delta = delta_t.reshape(width, rows, kl).transpose(2, 1, 0)
    return modes_now.astype(f32) + time_step * delta.astype(f32)


def with_halo(array, sides, width):
    for axis, dim in sides:
        peers, length = (lax.axis_size(axis), array.shape[dim])
        up = [(i, (i + 1) % peers) for i in range(peers - 1)]
        down = [(j, i) for i, j in up]
        last = lax.slice_in_dim(array, length - width, length, axis=dim)
        leading = lax.slice_in_dim(array, 0, width, axis=dim)
        before = lax.ppermute(last, axis, up)
        after = lax.ppermute(leading, axis, down)
        array = jnp.concatenate([before, array, after], axis=dim)
    return array


def neighbour(array, drow, dcol):
    return array[:, 1 + drow : array.shape[1] - 1 + drow, 1 + dcol : array.shape[2] - 1 + dcol]


def drive_with(field_ext, coeff_ext, rates, weights):
    center = neighbour(field_ext, 0, 0)
    coeff_mid = neighbour(coeff_ext, 0, 0)
    total = jnp.zeros_like(center)
    for drow, dcol in ((-1, 0), (1, 0), (0, -1), (0, 1)):
        total = total + (coeff_mid + neighbour(coeff_ext, drow, dcol)) * (
            neighbour(field_ext, drow, dcol) - center
        )
    total = total + rates[:, None, None] * (center - center * center * center)
    return (weights[:, None, None] * total).astype(jnp.bfloat16).reshape(center.shape[0], -1)


def rim_fields(field):
    return with_halo(field, (("gy", 1), ("gx", 2)), 1)


def body(modes_now, basis_rows, quad_weights, germ_nodes, log_fields, reaction_rates):
    k_local, rows_y, cols_x = modes_now.shape
    q_local, modes_total = basis_rows.shape
    log_ext = with_halo(log_fields, (("gy", 1), ("gx", 2)), 1)
    coeff_ext = jnp.exp(
        jnp.einsum("qj,jyx->qyx", germ_nodes, log_ext, precision=lax.Precision.HIGHEST)
    )

    def drive(field_ext):
        return drive_with(field_ext, coeff_ext, reaction_rates, quad_weights)

    current = modes_now.astype(jnp.float32)
    gathered = lax.all_gather(modes_now.reshape(k_local, -1), "quad", axis=0, tiled=True)
    field_zero = jnp.dot(basis_rows, gathered, preferred_element_type=jnp.float32)
    field_zero = rim_fields(field_zero.reshape(q_local, rows_y, cols_x))
    inner = gathered.reshape(modes_total, rows_y, cols_x)
    weighted_zero = drive(field_zero)
    partial_sum = lax.dot_general(
        basis_rows, weighted_zero, (((0,), (0,)), ((), ())), preferred_element_type=jnp.float32
    )
    summed = (
        lax.psum(partial_sum.astype(jnp.bfloat16), "quad")
        .astype(jnp.float32)
        .reshape(modes_total, rows_y, cols_x)
    )
    iterate_one = (inner.astype(jnp.float32) + time_step * summed).astype(jnp.bfloat16)
    flat = iterate_one.reshape(modes_total, -1)
    field_one = rim_fields(
        jnp.dot(basis_rows, flat, preferred_element_type=jnp.float32).reshape(
            q_local, rows_y, cols_x
        )
    )
    weighted = drive(field_one)
    second = (
        lax.psum_scatter(
            lax.dot_general(
                basis_rows, weighted, (((0,), (0,)), ((), ())), preferred_element_type=jnp.float32
            ).astype(jnp.bfloat16),
            "quad",
            scatter_dimension=0,
            tiled=True,
        )
        .astype(jnp.float32)
        .reshape(k_local, rows_y, cols_x)
    )
    return current + time_step * second


def solution(mesh):
    n, ny, nx = (mesh.shape[name] for name in ("quad", "gy", "gx"))
    planar = (ny, nx) == (2, 4) and n > 1
    run = functools.partial(fast_body, n, ny, nx) if planar else body
    in_specs = (
        P("quad", "gy", "gx"),
        P("quad", None),
        P("quad"),
        P("quad", None),
        P(None, "gy", "gx"),
        P("quad"),
    )
    out_specs = P("quad", "gy", "gx")
    return jax.shard_map(run, mesh=mesh, in_specs=in_specs, out_specs=out_specs, check_vma=False)
```

```python
import functools

import jax
import jax.numpy as jnp
from jax import lax
from jax.experimental import pallas as pl
from jax.experimental.pallas import tpu as pltpu
from jax.sharding import PartitionSpec as P

time_step = 0.04
LANES = 128
GROUP = 16
NODE_PARTS = (0, 0, 1, 1, 0, 2)
LOG_PARTS = (0, 1, 0, 1, 2, 0)
MESH = pl.DeviceIdType.MESH


def split_parts(values, pattern, axis):
    parts, rest = [], values
    for _ in range(3):
        part = rest.astype(jnp.bfloat16)
        parts.append(part.astype(jnp.float32))
        rest = rest - parts[-1]
    group = lax.broadcasted_iota(jnp.int32, values.shape, axis) // GROUP
    chosen = jnp.zeros_like(values)
    for index, which in enumerate(pattern):
        chosen = jnp.where(group == index, parts[which], chosen)
    return chosen.astype(jnp.bfloat16)


def spread(rows):
    def zeros(count):
        return jnp.zeros((count, rows.shape[1]), rows.dtype)

    copies = len(NODE_PARTS)
    one = jnp.concatenate([rows, zeros(GROUP - rows.shape[0])], axis=0)
    return jnp.concatenate([one] * copies + [zeros(LANES - copies * GROUP)], axis=0)


def dot_nt(a, b):
    return lax.dot_general(a, b, (((1,), (1,)), ((), ())), preferred_element_type=jnp.float32)


def dot_nn(a, b):
    return jnp.dot(a, b, preferred_element_type=jnp.float32)


def picard_kernel(
    dims, modes_ref, basis_ref, nodes_ref, weights_ref, rates_ref, logs_ref, out_ref,
    basis, first, second, halo_out, field_a, field_b, coeff, faces, weighted, outgoing, landed,
    local_sem, load_sem, b_send, b_recv, m_send, m_recv, h_send, h_recv, o_send, o_recv,
):
    n, ny, nx, kl, ql, terms, rows, cols, qb = dims
    modes, cells, rim = n * kl, rows * cols, 2 * rows
    quad_pts, piece = n * ql, ql // (ny * nx)
    z, gy, gx = lax.axis_index("quad"), lax.axis_index("gy"), lax.axis_index("gx")
    even = lax.rem(gx, 2) == 0
    other_gy = 1 - gy
    other_core = gx + 1 - 2 * lax.rem(gx, 2)
    other_x = lax.rem(gx + 2, 4)
    to_x, to_y, to_core = (z, gy, other_x), (z, other_gy, gx), (z, gy, other_core)
    own, edge = pl.ds(rim, cells), 2 * rim + cells

    def block_of(rank):
        return jnp.where(even, rank, n - 1 - rank)

    def remote(src, dst, send, recv, target):
        return pltpu.make_async_remote_copy(
            src_ref=src, dst_ref=dst, send_sem=send, recv_sem=recv,
            device_id=target, device_id_type=MESH,
        )

    barrier = pltpu.get_barrier_semaphore()
    for step in range(1, n):
        pl.semaphore_signal(barrier, inc=1, device_id=(lax.rem(z + step, n), gy, gx), device_id_type=MESH)
    for step in range(1, nx):
        pl.semaphore_signal(barrier, inc=1, device_id=(z, gy, lax.rem(gx + step, nx)), device_id_type=MESH)
    pl.semaphore_signal(barrier, inc=1, device_id=to_y, device_id_type=MESH)
    pl.semaphore_wait(barrier, n + nx - 1)

    def modes_copy(rank):
        rows_of = pl.multiple_of(block_of(rank) * cells, cells)
        return modes_ref.at[pl.ds(rows_of, cells), :]

    def modes_slot(rank):
        return first.at[own, pl.ds(pl.multiple_of(rank * kl, kl), kl)]

    def peer(step):
        return lax.rem(z + step, n)

    place = gy * nx + gx
    loads = []
    for step in range(ny * nx):
        offset = pl.multiple_of(lax.rem(place + step, ny * nx) * piece, piece)
        loads.append(
            pltpu.make_async_copy(
                basis_ref.at[pl.ds(offset, piece), :],
                basis.at[pl.ds(pl.multiple_of(z * ql + offset, piece), piece), pl.ds(0, modes)],
                load_sem.at[step],
            )
        )
        loads[-1].start()
    scalars_rows = jnp.concatenate([nodes_ref[...], weights_ref[...], rates_ref[...]], axis=0)
    basis[pl.ds(pl.multiple_of(z * ql, ql), ql), modes : modes + LANES] = split_parts(
        spread(scalars_rows).T, NODE_PARTS, 1
    )
    loads[0].wait()

    def rows_at(shard, y, x, part=None):
        start = shard * ql + (y * nx + x) * piece
        if part is None:
            return basis.at[pl.ds(pl.multiple_of(start, piece), piece), :]
        half = piece // 2
        return basis.at[pl.ds(pl.multiple_of(start + part * half, half), half), :]

    Z, X, Y, DA, DB, S0, SX, SY, SA, SB, ZB = range(11)

    def push(ref, shard, kind, target, send_kind=None):
        send_kind = kind if send_kind is None else send_kind
        return remote(ref, ref, b_send.at[shard, send_kind], b_recv.at[shard, kind], target)

    def arrived(ref, shard, kind):
        push(ref, shard, kind, to_core).wait_recv()

    def up(shard):
        return push(rows_at(shard, gy, gx), shard, Z, (jnp.minimum(z + 1, n - 1), gy, gx))

    def down(shard):
        return push(rows_at(shard, gy, gx), shard, Z, (jnp.maximum(z - 1, 0), gy, gx), ZB)

    @pl.when(z < n - 1)
    def _():
        up(z).start()

    @pl.when(z > 0)
    def _():
        down(z).start()

    for step in range(1, n):
        remote(modes_copy(peer(step)), modes_slot(z), m_send.at[step], m_recv.at[step], (peer(step), gy, gx)).start()
    load_modes = pltpu.make_async_copy(modes_copy(z), modes_slot(z), local_sem.at[0])
    load_modes.start()

    def plane(shard):
        mine = rows_at(shard, gy, gx)
        return [push(mine, shard, X, to_x), push(mine, shard, Y, to_y), push(mine, shard, S0, to_core)]

    def relay(shard):
        by_x, by_y = rows_at(shard, gy, other_x), rows_at(shard, other_gy, gx)
        return (
            [push(rows_at(shard, gy, other_x, 0), shard, DA, to_y), push(by_x, shard, SX, to_core)],
            [push(rows_at(shard, other_gy, gx, 1), shard, DB, to_x), push(by_y, shard, SY, to_core)],
        )

    def across(shard):
        return [
            push(rows_at(shard, other_gy, other_x, 0), shard, SA, to_core),
            push(rows_at(shard, other_gy, other_x, 1), shard, SB, to_core),
        ]

    def stage_z(shard):
        arrived(rows_at(shard, gy, gx), shard, Z)
        for copy in plane(shard):
            copy.start()

        @pl.when((shard < z) & (z < n - 1))
        def _():
            up(shard).start()

        @pl.when((shard > z) & (z > 0))
        def _():
            down(shard).start()

    def stage_xy(shard):
        after_x, after_y = relay(shard)
        arrived(rows_at(shard, gy, other_x), shard, X)
        for copy in after_x:
            copy.start()
        arrived(rows_at(shard, other_gy, gx), shard, Y)
        for copy in after_y:
            copy.start()

    def stage_d(shard):
        one, two = across(shard)
        arrived(rows_at(shard, other_gy, other_x, 0), shard, DA)
        one.start()
        arrived(rows_at(shard, other_gy, other_x, 1), shard, DB)
        two.start()

    def stage_s(shard):
        arrived(rows_at(shard, gy, other_core), shard, S0)
        core_x = lax.rem(other_core + 2, 4)
        arrived(rows_at(shard, gy, core_x), shard, SX)
        arrived(rows_at(shard, other_gy, other_core), shard, SY)
        arrived(rows_at(shard, other_gy, core_x, 0), shard, SA)
        arrived(rows_at(shard, other_gy, core_x, 1), shard, SB)

    def drain(shard):
        for copy in plane(shard) + relay(shard)[0] + relay(shard)[1] + across(shard):
            copy.wait_send()

        @pl.when((shard < z) & (z < n - 1))
        def _():
            up(shard).wait_send()

        @pl.when((shard > z) & (z > 0))
        def _():
            down(shard).wait_send()

    block = block_of(z)
    ahead = jnp.where(even, 1, -1)
    in_right, in_left = block < n - 1, block > 0
    has_right, has_left = in_right | (gx < nx - 1), in_left | (gx > 0)
    right_z, left_z = jnp.where(in_right, z + ahead, z), jnp.where(in_left, z - ahead, z)
    right_x = jnp.where(in_right, gx, jnp.minimum(gx + 1, nx - 1))
    left_x = jnp.where(in_left, gx, jnp.maximum(gx - 1, 0))

    def halo(turn, grid):
        width = grid.shape[1]
        span = pl.ds(0, width)
        hr, hs = h_recv, h_send
        lead, tail = grid.at[pl.ds(rim, rim), span], grid.at[pl.ds(cells, rim), span]
        before, after = grid.at[pl.ds(0, rim), span], grid.at[pl.ds(rim + cells, rim), span]
        top, bottom = grid.at[pl.ds(edge, cols), span], grid.at[pl.ds(edge + cols, cols), span]
        mine_last = halo_out.at[turn, pl.ds(0, cols), span]
        mine_lead = halo_out.at[turn, pl.ds(cols, cols), span]
        row = lax.broadcasted_iota(jnp.int32, (2 * cols, cells), 0)
        cell = lax.broadcasted_iota(jnp.int32, (2 * cols, cells), 1)
        wanted = jnp.where(row < cols, row * rows + rows - 1, (row - cols) * rows)
        pick = (wanted == cell).astype(jnp.float32).astype(jnp.bfloat16)

        steps = (
            (has_right, remote(tail, before, hs.at[turn, 0], hr.at[turn, 0], (right_z, gy, right_x)), has_left, before),
            (has_left, remote(lead, after, hs.at[turn, 1], hr.at[turn, 1], (left_z, gy, left_x)), has_right, after),
            (gy < ny - 1, remote(mine_last, top, hs.at[turn, 2], hr.at[turn, 2], to_y), gy > 0, top),
            (gy > 0, remote(mine_lead, bottom, hs.at[turn, 3], hr.at[turn, 3], to_y), gy < ny - 1, bottom),
        )

        def start():
            halo_out[turn, :, 0:width] = dot_nn(pick, grid[rim : rim + cells, :]).astype(jnp.bfloat16)
            for sends, copy, gets, slot in steps:

                @pl.when(sends)
                def _():
                    copy.start()

                @pl.when(jnp.logical_not(gets))
                def _():
                    slot[...] = jnp.zeros(slot.shape, jnp.bfloat16)

        def finish():
            for sends, copy, gets, slot in steps:

                @pl.when(gets)
                def _():
                    copy.wait_recv()

        def drained():
            for sends, copy, gets, slot in steps:

                @pl.when(sends)
                def _():
                    copy.wait_send()

        return start, finish, drained

    lane = lax.broadcasted_iota(jnp.int32, (GROUP, LANES), 1)
    line = lax.broadcasted_iota(jnp.int32, (GROUP, LANES), 0)
    group = lane // GROUP
    whole = (group == 0) | (group == 2) | (group == 5)
    wants = (lane - group * GROUP) == terms + line
    select = jnp.where(whole & wants & (line < 2), 1.0, 0.0).astype(jnp.bfloat16)
    lanes = min(256, qb)
    slab = 2 * rows

    def start_of(block_index):
        return pl.multiple_of(block_index * qb, qb)

    def multiply(field, block_index, grid):
        field[...] = dot_nt(grid[:, 0:modes], basis[pl.ds(start_of(block_index), qb), 0:modes])

    def drive(field, block_index, fresh):
        start = start_of(block_index)
        ext = basis[pl.ds(start, qb), modes : modes + LANES]
        scalars = dot_nt(select, ext)
        if fresh:
            coeff[...] = jnp.exp(dot_nt(first[:, modes : modes + LANES], ext))
        y_at = lax.broadcasted_iota(jnp.int32, (rows, lanes), 0)
        for h in range(qb // lanes):
            part = slice(h * lanes, (h + 1) * lanes)
            here = pl.ds(start + h * lanes, lanes)
            weight, rate = scalars[0:1, part], scalars[1:2, part]

            def sides(ref, column):
                low = rim + column * rows
                mid = ref[low : low + rows, part]
                above = ref[edge + column : edge + column + 1, part]
                below = ref[edge + cols + column : edge + cols + column + 1, part]
                return mid, (
                    ref[low - rows : low, part],
                    ref[low + rows : low + 2 * rows, part],
                    jnp.where(y_at == 0, above, pltpu.roll(mid, 1, 0)),
                    jnp.where(y_at == rows - 1, below, pltpu.roll(mid, rows - 1, 0)),
                )

            for c in range(cols // 2):
                results = []
                for column in (2 * c, 2 * c + 1):
                    at = slice(column * rows, (column + 1) * rows)
                    mid, around = sides(field, column)
                    if fresh:
                        cm, others = sides(coeff, column)
                        sums = [cm + other for other in others]
                        for side, value in enumerate(sums):
                            faces[side, at, here] = value
                    else:
                        sums = [faces[side, at, here] for side in range(4)]
                    total = rate * (mid - mid * mid * mid)
                    for value, other in zip(sums, around):
                        total += value * (other - mid)
                    results.append(weight * total)
                weighted[c * slab : (c + 1) * slab, here] = jnp.concatenate(results, axis=0).astype(
                    jnp.bfloat16
                )

    per_shard = ql // qb
    fields = (field_a, field_b)

    def drive_shard(shard, between):
        base = shard * per_shard
        multiply(fields[0], base, first)
        for i in range(per_shard):
            if i + 1 < per_shard:
                multiply(fields[(i + 1) % 2], base + i + 1, first)
            drive(fields[i % 2], base + i, True)
            if i == 0:
                for call in between:
                    call()

    def drive_all():
        count = n * per_shard

        def pair(i, _):
            multiply(field_b, 2 * i + 1, second)
            drive(field_a, 2 * i, False)
            multiply(field_a, jnp.minimum(2 * i + 2, count - 1), second)
            drive(field_b, 2 * i + 1, False)
            return 0

        multiply(field_a, 0, second)
        lax.fori_loop(0, count // 2, pair, 0)

    cell_at = lax.broadcasted_iota(jnp.int32, (cells, logs_ref.shape[2]), 0)
    x_at = lax.broadcasted_iota(jnp.int32, (cells, logs_ref.shape[2]), 1) - block * cols
    logs = jnp.zeros((cells, LANES), jnp.float32)
    for y in range(rows):
        take = (cell_at == x_at * rows + y).astype(jnp.float32).astype(jnp.bfloat16)
        logs += dot_nt(take, split_parts(spread(logs_ref[:, y, :]), LOG_PARTS, 0))
    first[own, modes : modes + LANES] = logs.astype(jnp.bfloat16)
    halo_a = halo(0, first)

    def nth(j):
        shard = jnp.int32(0)
        for rank in range(n):
            order = sorted((s for s in range(n) if s != rank), key=lambda s: (abs(s - rank), s))
            shard = shard + jnp.where(z == rank, order[j], 0)
        return shard

    shards = [nth(j) for j in range(n - 1)]
    stages = (stage_z, stage_xy, stage_d)

    def turn_stages(turn):
        calls = []
        for depth, stage in reversed(list(enumerate(stages))):
            if 0 <= turn - depth < n - 1:
                calls.append(functools.partial(stage, shards[turn - depth]))
        return calls

    for call in turn_stages(0) + turn_stages(1):
        call()
    for load in loads[1:]:
        load.wait()
    load_modes.wait()
    for step in range(1, n):
        source = lax.rem(z - step + n, n)
        remote(modes_slot(source), modes_slot(source), m_send.at[step], m_recv.at[step], to_y).wait_recv()
    halo_a[0]()
    early = turn_stages(2)
    for call in early[:-1]:
        call()
    halo_a[1]()
    drive_shard(z, early[-1:])
    for j in range(n - 1):
        stage_s(shards[j])
        drive_shard(shards[j], turn_stages(j + 3))

    def project(rank):
        span = pl.ds(pl.multiple_of(rank * kl, kl), kl)
        return span, dot_nn(weighted[...], basis[:, span])

    def update(rank, _):
        span, got = project(rank)
        now = first[own, span].astype(jnp.float32)
        second[own, span] = (now + time_step * got).astype(jnp.bfloat16)
        return 0

    lax.fori_loop(0, n, update, 0)

    halo_b = halo(1, second)
    halo_b[0]()
    halo_b[1]()
    drive_all()

    def landing(owner_block):
        return landed.at[pl.ds(pl.multiple_of(owner_block * cells, cells), cells), :]

    def deliver(step):
        return remote(
            outgoing.at[step], landing(block), o_send.at[step], o_recv.at[step], (peer(step), gy, gx)
        )

    for step in range(1, n):
        outgoing[step] = project(peer(step))[1].astype(jnp.bfloat16)
        deliver(step).start()
    landed[pl.ds(pl.multiple_of(block * cells, cells), cells), :] = project(z)[1].astype(jnp.bfloat16)
    for step in range(1, n):
        source = landing(block_of(lax.rem(z - step + n, n)))
        remote(source, source, o_send.at[step], o_recv.at[step], to_y).wait_recv()
    out_ref[...] = landed[...]

    for step in range(1, n):
        deliver(step).wait_send()
        remote(modes_copy(peer(step)), modes_slot(z), m_send.at[step], m_recv.at[step], (peer(step), gy, gx)).wait_send()
    halo_a[2]()
    halo_b[2]()

    @pl.when(z < n - 1)
    def _():
        up(z).wait_send()

    @pl.when(z > 0)
    def _():
        down(z).wait_send()

    for shard in shards:
        drain(shard)


def fast_body(n, ny, nx, modes_now, basis_rows, quad_weights, germ_nodes, log_fields, reaction_rates):
    kl, rows, width = modes_now.shape
    ql, modes = basis_rows.shape
    terms = germ_nodes.shape[1]
    cols = width // n
    cells, tile, rim, quad_pts = rows * cols, rows * width, 2 * rows, n * ql
    qb = min(512, ql)
    ext = modes + LANES
    dims = (n, ny, nx, kl, ql, terms, rows, cols, qb)
    modes_t = modes_now.transpose(2, 1, 0).reshape(tile, kl)
    any_spec, vmem = pl.BlockSpec(memory_space=pl.ANY), pl.BlockSpec(memory_space=pltpu.VMEM)
    grid_rows = 2 * rim + cells + 2 * cols
    bf16, f32 = jnp.bfloat16, jnp.float32
    dma = pltpu.SemaphoreType.DMA
    delta_t = pl.pallas_call(
        functools.partial(picard_kernel, dims),
        out_shape=jax.ShapeDtypeStruct((tile, kl), bf16),
        in_specs=[any_spec, any_spec, vmem, vmem, vmem, vmem],
        out_specs=vmem,
        scratch_shapes=[
            pltpu.VMEM((quad_pts, ext), bf16),
            pltpu.VMEM((grid_rows, ext), bf16),
            pltpu.VMEM((grid_rows, modes), bf16),
            pltpu.VMEM((2, 2 * cols, ext), bf16),
            pltpu.VMEM((grid_rows, qb), f32),
            pltpu.VMEM((grid_rows, qb), f32),
            pltpu.VMEM((grid_rows, qb), f32),
            pltpu.VMEM((4, cells, quad_pts), f32),
            pltpu.VMEM((cells, quad_pts), bf16),
            pltpu.VMEM((n, cells, kl), bf16),
            pltpu.VMEM((tile, kl), bf16),
            dma((1,)),
            dma((ny * nx,)),
            dma((n, 11)),
            dma((n, 11)),
            dma((n,)),
            dma((n,)),
            dma((2, 4)),
            dma((2, 4)),
            dma((n,)),
            dma((n,)),
        ],
        compiler_params=pltpu.CompilerParams(
            collective_id=0, has_side_effects=True, vmem_limit_bytes=48 * 1024 * 1024
        ),
    )(modes_t, basis_rows, germ_nodes.T, quad_weights[None], reaction_rates[None], log_fields)
    delta = delta_t.reshape(width, rows, kl).transpose(2, 1, 0)
    return modes_now.astype(f32) + time_step * delta.astype(f32)


def with_halo(array, sides, width):
    for axis, dim in sides:
        peers, length = (lax.axis_size(axis), array.shape[dim])
        up = [(i, (i + 1) % peers) for i in range(peers - 1)]
        down = [(j, i) for i, j in up]
        last = lax.slice_in_dim(array, length - width, length, axis=dim)
        leading = lax.slice_in_dim(array, 0, width, axis=dim)
        before = lax.ppermute(last, axis, up)
        after = lax.ppermute(leading, axis, down)
        array = jnp.concatenate([before, array, after], axis=dim)
    return array


def neighbour(array, drow, dcol):
    return array[:, 1 + drow : array.shape[1] - 1 + drow, 1 + dcol : array.shape[2] - 1 + dcol]


def drive_with(field_ext, coeff_ext, rates, weights):
    center = neighbour(field_ext, 0, 0)
    coeff_mid = neighbour(coeff_ext, 0, 0)
    total = jnp.zeros_like(center)
    for drow, dcol in ((-1, 0), (1, 0), (0, -1), (0, 1)):
        total = total + (coeff_mid + neighbour(coeff_ext, drow, dcol)) * (
            neighbour(field_ext, drow, dcol) - center
        )
    total = total + rates[:, None, None] * (center - center * center * center)
    return (weights[:, None, None] * total).astype(jnp.bfloat16).reshape(center.shape[0], -1)


def rim_fields(field):
    return with_halo(field, (("gy", 1), ("gx", 2)), 1)


def body(modes_now, basis_rows, quad_weights, germ_nodes, log_fields, reaction_rates):
    k_local, rows_y, cols_x = modes_now.shape
    q_local, modes_total = basis_rows.shape
    log_ext = with_halo(log_fields, (("gy", 1), ("gx", 2)), 1)
    coeff_ext = jnp.exp(
        jnp.einsum("qj,jyx->qyx", germ_nodes, log_ext, precision=lax.Precision.HIGHEST)
    )

    def drive(field_ext):
        return drive_with(field_ext, coeff_ext, reaction_rates, quad_weights)

    current = modes_now.astype(jnp.float32)
    gathered = lax.all_gather(modes_now.reshape(k_local, -1), "quad", axis=0, tiled=True)
    field_zero = jnp.dot(basis_rows, gathered, preferred_element_type=jnp.float32)
    field_zero = rim_fields(field_zero.reshape(q_local, rows_y, cols_x))
    inner = gathered.reshape(modes_total, rows_y, cols_x)
    weighted_zero = drive(field_zero)
    partial_sum = lax.dot_general(
        basis_rows, weighted_zero, (((0,), (0,)), ((), ())), preferred_element_type=jnp.float32
    )
    summed = (
        lax.psum(partial_sum.astype(jnp.bfloat16), "quad")
        .astype(jnp.float32)
        .reshape(modes_total, rows_y, cols_x)
    )
    iterate_one = (inner.astype(jnp.float32) + time_step * summed).astype(jnp.bfloat16)
    flat = iterate_one.reshape(modes_total, -1)
    field_one = rim_fields(
        jnp.dot(basis_rows, flat, preferred_element_type=jnp.float32).reshape(
            q_local, rows_y, cols_x
        )
    )
    weighted = drive(field_one)
    second = (
        lax.psum_scatter(
            lax.dot_general(
                basis_rows, weighted, (((0,), (0,)), ((), ())), preferred_element_type=jnp.float32
            ).astype(jnp.bfloat16),
            "quad",
            scatter_dimension=0,
            tiled=True,
        )
        .astype(jnp.float32)
        .reshape(k_local, rows_y, cols_x)
    )
    return current + time_step * second


def solution(mesh):
    n, ny, nx = (mesh.shape[name] for name in ("quad", "gy", "gx"))
    planar = (ny, nx) == (2, 4) and n > 1
    run = functools.partial(fast_body, n, ny, nx) if planar else body
    in_specs = (
        P("quad", "gy", "gx"),
        P("quad", None),
        P("quad"),
        P("quad", None),
        P(None, "gy", "gx"),
        P("quad"),
    )
    out_specs = P("quad", "gy", "gx")
    return jax.shard_map(run, mesh=mesh, in_specs=in_specs, out_specs=out_specs, check_vma=False)
```

```python
import functools

import jax
import jax.numpy as jnp
from jax import lax
from jax.experimental import pallas as pl
from jax.experimental.pallas import tpu as pltpu
from jax.sharding import PartitionSpec as P

time_step = 0.04
LANES = 128
GROUP = 16
NODE_PARTS = (0, 0, 1, 1, 0, 2)
LOG_PARTS = (0, 1, 0, 1, 2, 0)
MESH = pl.DeviceIdType.MESH


def split_parts(values, pattern, axis):
    parts, rest = [], values
    for _ in range(3):
        part = rest.astype(jnp.bfloat16)
        parts.append(part.astype(jnp.float32))
        rest = rest - parts[-1]
    group = lax.broadcasted_iota(jnp.int32, values.shape, axis) // GROUP
    chosen = jnp.zeros_like(values)
    for index, which in enumerate(pattern):
        chosen = jnp.where(group == index, parts[which], chosen)
    return chosen.astype(jnp.bfloat16)


def spread(rows):
    def zeros(count):
        return jnp.zeros((count, rows.shape[1]), rows.dtype)

    copies = len(NODE_PARTS)
    one = jnp.concatenate([rows, zeros(GROUP - rows.shape[0])], axis=0)
    return jnp.concatenate([one] * copies + [zeros(LANES - copies * GROUP)], axis=0)


def dot_nt(a, b):
    return lax.dot_general(a, b, (((1,), (1,)), ((), ())), preferred_element_type=jnp.float32)


def dot_nn(a, b):
    return jnp.dot(a, b, preferred_element_type=jnp.float32)


def picard_kernel(
    dims, modes_ref, basis_ref, nodes_ref, weights_ref, rates_ref, logs_ref, out_ref,
    basis, first, second, halo_out, field_a, field_b, coeff, faces, weighted, outgoing, landed,
    local_sem, load_sem, b_send, b_recv, m_send, m_recv, h_send, h_recv, o_send, o_recv,
):
    n, ny, nx, kl, ql, terms, rows, cols, qb = dims
    modes, cells, rim = n * kl, rows * cols, 2 * rows
    quad_pts, piece = n * ql, ql // (ny * nx)
    z, gy, gx = lax.axis_index("quad"), lax.axis_index("gy"), lax.axis_index("gx")
    even = lax.rem(gx, 2) == 0
    other_gy = 1 - gy
    other_core = gx + 1 - 2 * lax.rem(gx, 2)
    other_x = lax.rem(gx + 2, 4)
    to_x, to_y, to_core = (z, gy, other_x), (z, other_gy, gx), (z, gy, other_core)
    own, edge = pl.ds(rim, cells), 2 * rim + cells

    def block_of(rank):
        return jnp.where(even, rank, n - 1 - rank)

    def remote(src, dst, send, recv, target):
        return pltpu.make_async_remote_copy(
            src_ref=src, dst_ref=dst, send_sem=send, recv_sem=recv,
            device_id=target, device_id_type=MESH,
        )

    barrier = pltpu.get_barrier_semaphore()
    for step in range(1, n):
        pl.semaphore_signal(barrier, inc=1, device_id=(lax.rem(z + step, n), gy, gx), device_id_type=MESH)
    for step in range(1, nx):
        pl.semaphore_signal(barrier, inc=1, device_id=(z, gy, lax.rem(gx + step, nx)), device_id_type=MESH)
    pl.semaphore_signal(barrier, inc=1, device_id=to_y, device_id_type=MESH)
    pl.semaphore_wait(barrier, n + nx - 1)

    def modes_copy(rank):
        rows_of = pl.multiple_of(block_of(rank) * cells, cells)
        return modes_ref.at[pl.ds(rows_of, cells), :]

    def modes_slot(rank):
        return first.at[own, pl.ds(pl.multiple_of(rank * kl, kl), kl)]

    def peer(step):
        return lax.rem(z + step, n)

    place = gy * nx + gx
    loads = []
    for step in range(ny * nx):
        offset = pl.multiple_of(lax.rem(place + step, ny * nx) * piece, piece)
        loads.append(
            pltpu.make_async_copy(
                basis_ref.at[pl.ds(offset, piece), :],
                basis.at[pl.ds(pl.multiple_of(z * ql + offset, piece), piece), pl.ds(0, modes)],
                load_sem.at[step],
            )
        )
        loads[-1].start()
    scalars_rows = jnp.concatenate([nodes_ref[...], weights_ref[...], rates_ref[...]], axis=0)
    basis[pl.ds(pl.multiple_of(z * ql, ql), ql), modes : modes + LANES] = split_parts(
        spread(scalars_rows).T, NODE_PARTS, 1
    )
    loads[0].wait()

    def rows_at(shard, y, x, part=None):
        start = shard * ql + (y * nx + x) * piece
        if part is None:
            return basis.at[pl.ds(pl.multiple_of(start, piece), piece), :]
        half = piece // 2
        return basis.at[pl.ds(pl.multiple_of(start + part * half, half), half), :]

    Z, X, Y, ZB = (0, 1), (2, 3), (4, 5), (6, 7)
    DA, DB, S0, SX, SY, SA, SB = range(8, 15)

    def push(ref, shard, kind, target, send_kind=None):
        send_kind = kind if send_kind is None else send_kind
        return remote(ref, ref, b_send.at[shard, send_kind], b_recv.at[shard, kind], target)

    def arrived(ref, shard, kind):
        push(ref, shard, kind, to_core).wait_recv()

    def up(shard, part):
        target = (jnp.minimum(z + 1, n - 1), gy, gx)
        return push(rows_at(shard, gy, gx, part), shard, Z[part], target)

    def down(shard, part):
        target = (jnp.maximum(z - 1, 0), gy, gx)
        return push(rows_at(shard, gy, gx, part), shard, Z[part], target, ZB[part])

    @pl.when(z < n - 1)
    def _():
        for part in (0, 1):
            up(z, part).start()

    @pl.when(z > 0)
    def _():
        for part in (0, 1):
            down(z, part).start()

    for step in range(1, n):
        remote(modes_copy(peer(step)), modes_slot(z), m_send.at[step], m_recv.at[step], (peer(step), gy, gx)).start()
    load_modes = pltpu.make_async_copy(modes_copy(z), modes_slot(z), local_sem.at[0])
    load_modes.start()

    def plane(shard, part):
        mine = rows_at(shard, gy, gx, part)
        return [push(mine, shard, X[part], to_x), push(mine, shard, Y[part], to_y)]

    def to_sibling(shard):
        return push(rows_at(shard, gy, gx), shard, S0, to_core)

    def relay(shard):
        by_x, by_y = rows_at(shard, gy, other_x), rows_at(shard, other_gy, gx)
        return (
            [push(rows_at(shard, gy, other_x, 0), shard, DA, to_y), push(by_x, shard, SX, to_core)],
            [push(rows_at(shard, other_gy, gx, 1), shard, DB, to_x), push(by_y, shard, SY, to_core)],
        )

    def across(shard):
        return [
            push(rows_at(shard, other_gy, other_x, 0), shard, SA, to_core),
            push(rows_at(shard, other_gy, other_x, 1), shard, SB, to_core),
        ]

    def stage_z(shard):
        for part in (0, 1):
            arrived(rows_at(shard, gy, gx, part), shard, Z[part])

            @pl.when((shard < z) & (z < n - 1))
            def _():
                up(shard, part).start()

            @pl.when((shard > z) & (z > 0))
            def _():
                down(shard, part).start()

            for copy in plane(shard, part):
                copy.start()
        to_sibling(shard).start()

    def stage_xy(shard):
        after_x, after_y = relay(shard)
        arrived(rows_at(shard, gy, other_x, 0), shard, X[0])
        after_x[0].start()
        arrived(rows_at(shard, gy, other_x, 1), shard, X[1])
        after_x[1].start()
        arrived(rows_at(shard, other_gy, gx, 0), shard, Y[0])
        arrived(rows_at(shard, other_gy, gx, 1), shard, Y[1])
        for copy in after_y:
            copy.start()

    def stage_d(shard):
        one, two = across(shard)
        arrived(rows_at(shard, other_gy, other_x, 0), shard, DA)
        one.start()
        arrived(rows_at(shard, other_gy, other_x, 1), shard, DB)
        two.start()

    def stage_s(shard):
        arrived(rows_at(shard, gy, other_core), shard, S0)
        core_x = lax.rem(other_core + 2, 4)
        arrived(rows_at(shard, gy, core_x), shard, SX)
        arrived(rows_at(shard, other_gy, other_core), shard, SY)
        arrived(rows_at(shard, other_gy, core_x, 0), shard, SA)
        arrived(rows_at(shard, other_gy, core_x, 1), shard, SB)

    def drain(shard):
        copies = plane(shard, 0) + plane(shard, 1) + [to_sibling(shard)]
        for copy in copies + relay(shard)[0] + relay(shard)[1] + across(shard):
            copy.wait_send()
        for part in (0, 1):

            @pl.when((shard < z) & (z < n - 1))
            def _():
                up(shard, part).wait_send()

            @pl.when((shard > z) & (z > 0))
            def _():
                down(shard, part).wait_send()

    block = block_of(z)
    ahead = jnp.where(even, 1, -1)
    in_right, in_left = block < n - 1, block > 0
    has_right, has_left = in_right | (gx < nx - 1), in_left | (gx > 0)
    right_z, left_z = jnp.where(in_right, z + ahead, z), jnp.where(in_left, z - ahead, z)
    right_x = jnp.where(in_right, gx, jnp.minimum(gx + 1, nx - 1))
    left_x = jnp.where(in_left, gx, jnp.maximum(gx - 1, 0))

    def halo(turn, grid):
        width = grid.shape[1]
        span = pl.ds(0, width)
        hr, hs = h_recv, h_send
        lead, tail = grid.at[pl.ds(rim, rim), span], grid.at[pl.ds(cells, rim), span]
        before, after = grid.at[pl.ds(0, rim), span], grid.at[pl.ds(rim + cells, rim), span]
        top, bottom = grid.at[pl.ds(edge, cols), span], grid.at[pl.ds(edge + cols, cols), span]
        mine_last = halo_out.at[turn, pl.ds(0, cols), span]
        mine_lead = halo_out.at[turn, pl.ds(cols, cols), span]
        row = lax.broadcasted_iota(jnp.int32, (2 * cols, cells), 0)
        cell = lax.broadcasted_iota(jnp.int32, (2 * cols, cells), 1)
        wanted = jnp.where(row < cols, row * rows + rows - 1, (row - cols) * rows)
        pick = (wanted == cell).astype(jnp.float32).astype(jnp.bfloat16)

        steps = (
            (has_right, remote(tail, before, hs.at[turn, 0], hr.at[turn, 0], (right_z, gy, right_x)), has_left, before),
            (has_left, remote(lead, after, hs.at[turn, 1], hr.at[turn, 1], (left_z, gy, left_x)), has_right, after),
            (gy < ny - 1, remote(mine_last, top, hs.at[turn, 2], hr.at[turn, 2], to_y), gy > 0, top),
            (gy > 0, remote(mine_lead, bottom, hs.at[turn, 3], hr.at[turn, 3], to_y), gy < ny - 1, bottom),
        )

        def start():
            halo_out[turn, :, 0:width] = dot_nn(pick, grid[rim : rim + cells, :]).astype(jnp.bfloat16)
            for sends, copy, gets, slot in steps:

                @pl.when(sends)
                def _():
                    copy.start()

                @pl.when(jnp.logical_not(gets))
                def _():
                    slot[...] = jnp.zeros(slot.shape, jnp.bfloat16)

        def finish():
            for sends, copy, gets, slot in steps:

                @pl.when(gets)
                def _():
                    copy.wait_recv()

        def drained():
            for sends, copy, gets, slot in steps:

                @pl.when(sends)
                def _():
                    copy.wait_send()

        return start, finish, drained

    lane = lax.broadcasted_iota(jnp.int32, (GROUP, LANES), 1)
    line = lax.broadcasted_iota(jnp.int32, (GROUP, LANES), 0)
    group = lane // GROUP
    whole = (group == 0) | (group == 2) | (group == 5)
    wants = (lane - group * GROUP) == terms + line
    select = jnp.where(whole & wants & (line < 2), 1.0, 0.0).astype(jnp.bfloat16)
    lanes = min(256, qb)
    slab = 2 * rows

    def start_of(block_index):
        return pl.multiple_of(block_index * qb, qb)

    def multiply(field, block_index, grid):
        field[...] = dot_nt(grid[:, 0:modes], basis[pl.ds(start_of(block_index), qb), 0:modes])

    def drive(field, block_index, fresh):
        start = start_of(block_index)
        ext = basis[pl.ds(start, qb), modes : modes + LANES]
        scalars = dot_nt(select, ext)
        if fresh:
            coeff[...] = jnp.exp(dot_nt(first[:, modes : modes + LANES], ext))
        y_at = lax.broadcasted_iota(jnp.int32, (rows, lanes), 0)
        for h in range(qb // lanes):
            part = slice(h * lanes, (h + 1) * lanes)
            here = pl.ds(start + h * lanes, lanes)
            weight, rate = scalars[0:1, part], scalars[1:2, part]

            def sides(ref, column):
                low = rim + column * rows
                mid = ref[low : low + rows, part]
                above = ref[edge + column : edge + column + 1, part]
                below = ref[edge + cols + column : edge + cols + column + 1, part]
                return mid, (
                    ref[low - rows : low, part],
                    ref[low + rows : low + 2 * rows, part],
                    jnp.where(y_at == 0, above, pltpu.roll(mid, 1, 0)),
                    jnp.where(y_at == rows - 1, below, pltpu.roll(mid, rows - 1, 0)),
                )

            for c in range(cols // 2):
                results = []
                for column in (2 * c, 2 * c + 1):
                    at = slice(column * rows, (column + 1) * rows)
                    mid, around = sides(field, column)
                    if fresh:
                        cm, others = sides(coeff, column)
                        sums = [cm + other for other in others]
                        for side, value in enumerate(sums):
                            faces[side, at, here] = value
                    else:
                        sums = [faces[side, at, here] for side in range(4)]
                    total = rate * (mid - mid * mid * mid)
                    for value, other in zip(sums, around):
                        total += value * (other - mid)
                    results.append(weight * total)
                weighted[c * slab : (c + 1) * slab, here] = jnp.concatenate(results, axis=0).astype(
                    jnp.bfloat16
                )

    per_shard = ql // qb
    fields = (field_a, field_b)

    def drive_shard(shard, between):
        base = shard * per_shard
        multiply(fields[0], base, first)
        for i in range(per_shard):
            if i + 1 < per_shard:
                multiply(fields[(i + 1) % 2], base + i + 1, first)
            drive(fields[i % 2], base + i, True)
            if i == 0:
                for call in between:
                    call()

    def drive_all():
        count = n * per_shard

        def pair(i, _):
            multiply(field_b, 2 * i + 1, second)
            drive(field_a, 2 * i, False)
            multiply(field_a, jnp.minimum(2 * i + 2, count - 1), second)
            drive(field_b, 2 * i + 1, False)
            return 0

        multiply(field_a, 0, second)
        lax.fori_loop(0, count // 2, pair, 0)

    cell_at = lax.broadcasted_iota(jnp.int32, (cells, logs_ref.shape[2]), 0)
    x_at = lax.broadcasted_iota(jnp.int32, (cells, logs_ref.shape[2]), 1) - block * cols
    logs = jnp.zeros((cells, LANES), jnp.float32)
    for y in range(rows):
        take = (cell_at == x_at * rows + y).astype(jnp.float32).astype(jnp.bfloat16)
        logs += dot_nt(take, split_parts(spread(logs_ref[:, y, :]), LOG_PARTS, 0))
    first[own, modes : modes + LANES] = logs.astype(jnp.bfloat16)
    halo_a = halo(0, first)

    def nth(j):
        shard = jnp.int32(0)
        for rank in range(n):
            order = sorted((s for s in range(n) if s != rank), key=lambda s: (abs(s - rank), s))
            shard = shard + jnp.where(z == rank, order[j], 0)
        return shard

    shards = [nth(j) for j in range(n - 1)]
    stages = (stage_z, stage_xy, stage_d)

    def turn_stages(turn):
        calls = []
        for depth, stage in reversed(list(enumerate(stages))):
            if 0 <= turn - depth < n - 1:
                calls.append(functools.partial(stage, shards[turn - depth]))
        return calls

    for call in turn_stages(0) + turn_stages(1):
        call()
    for load in loads[1:]:
        load.wait()
    load_modes.wait()
    for step in range(1, n):
        source = lax.rem(z - step + n, n)
        remote(modes_slot(source), modes_slot(source), m_send.at[step], m_recv.at[step], to_y).wait_recv()
    halo_a[0]()
    early = turn_stages(2)
    for call in early[:-1]:
        call()
    halo_a[1]()
    drive_shard(z, early[-1:])
    for j in range(n - 1):
        stage_s(shards[j])
        drive_shard(shards[j], turn_stages(j + 3))

    def project(rank):
        span = pl.ds(pl.multiple_of(rank * kl, kl), kl)
        return span, dot_nn(weighted[...], basis[:, span])

    def update(rank, _):
        span, got = project(rank)
        now = first[own, span].astype(jnp.float32)
        second[own, span] = (now + time_step * got).astype(jnp.bfloat16)
        return 0

    lax.fori_loop(0, n, update, 0)

    halo_b = halo(1, second)
    halo_b[0]()
    halo_b[1]()
    drive_all()

    def landing(owner_block):
        return landed.at[pl.ds(pl.multiple_of(owner_block * cells, cells), cells), :]

    def deliver(step):
        return remote(
            outgoing.at[step], landing(block), o_send.at[step], o_recv.at[step], (peer(step), gy, gx)
        )

    for step in range(1, n):
        outgoing[step] = project(peer(step))[1].astype(jnp.bfloat16)
        deliver(step).start()
    landed[pl.ds(pl.multiple_of(block * cells, cells), cells), :] = project(z)[1].astype(jnp.bfloat16)
    for step in range(1, n):
        source = landing(block_of(lax.rem(z - step + n, n)))
        remote(source, source, o_send.at[step], o_recv.at[step], to_y).wait_recv()
    out_ref[...] = landed[...]

    for step in range(1, n):
        deliver(step).wait_send()
        remote(modes_copy(peer(step)), modes_slot(z), m_send.at[step], m_recv.at[step], (peer(step), gy, gx)).wait_send()
    halo_a[2]()
    halo_b[2]()

    for part in (0, 1):

        @pl.when(z < n - 1)
        def _():
            up(z, part).wait_send()

        @pl.when(z > 0)
        def _():
            down(z, part).wait_send()

    for shard in shards:
        drain(shard)


def fast_body(n, ny, nx, modes_now, basis_rows, quad_weights, germ_nodes, log_fields, reaction_rates):
    kl, rows, width = modes_now.shape
    ql, modes = basis_rows.shape
    terms = germ_nodes.shape[1]
    cols = width // n
    cells, tile, rim, quad_pts = rows * cols, rows * width, 2 * rows, n * ql
    qb = min(512, ql)
    ext = modes + LANES
    dims = (n, ny, nx, kl, ql, terms, rows, cols, qb)
    modes_t = modes_now.transpose(2, 1, 0).reshape(tile, kl)
    any_spec, vmem = pl.BlockSpec(memory_space=pl.ANY), pl.BlockSpec(memory_space=pltpu.VMEM)
    grid_rows = 2 * rim + cells + 2 * cols
    bf16, f32 = jnp.bfloat16, jnp.float32
    dma = pltpu.SemaphoreType.DMA
    delta_t = pl.pallas_call(
        functools.partial(picard_kernel, dims),
        out_shape=jax.ShapeDtypeStruct((tile, kl), bf16),
        in_specs=[any_spec, any_spec, vmem, vmem, vmem, vmem],
        out_specs=vmem,
        scratch_shapes=[
            pltpu.VMEM((quad_pts, ext), bf16),
            pltpu.VMEM((grid_rows, ext), bf16),
            pltpu.VMEM((grid_rows, modes), bf16),
            pltpu.VMEM((2, 2 * cols, ext), bf16),
            pltpu.VMEM((grid_rows, qb), f32),
            pltpu.VMEM((grid_rows, qb), f32),
            pltpu.VMEM((grid_rows, qb), f32),
            pltpu.VMEM((4, cells, quad_pts), f32),
            pltpu.VMEM((cells, quad_pts), bf16),
            pltpu.VMEM((n, cells, kl), bf16),
            pltpu.VMEM((tile, kl), bf16),
            dma((1,)),
            dma((ny * nx,)),
            dma((n, 15)),
            dma((n, 15)),
            dma((n,)),
            dma((n,)),
            dma((2, 4)),
            dma((2, 4)),
            dma((n,)),
            dma((n,)),
        ],
        compiler_params=pltpu.CompilerParams(
            collective_id=0, has_side_effects=True, vmem_limit_bytes=48 * 1024 * 1024
        ),
    )(modes_t, basis_rows, germ_nodes.T, quad_weights[None], reaction_rates[None], log_fields)
    delta = delta_t.reshape(width, rows, kl).transpose(2, 1, 0)
    return modes_now.astype(f32) + time_step * delta.astype(f32)


def with_halo(array, sides, width):
    for axis, dim in sides:
        peers, length = (lax.axis_size(axis), array.shape[dim])
        up = [(i, (i + 1) % peers) for i in range(peers - 1)]
        down = [(j, i) for i, j in up]
        last = lax.slice_in_dim(array, length - width, length, axis=dim)
        leading = lax.slice_in_dim(array, 0, width, axis=dim)
        before = lax.ppermute(last, axis, up)
        after = lax.ppermute(leading, axis, down)
        array = jnp.concatenate([before, array, after], axis=dim)
    return array


def neighbour(array, drow, dcol):
    return array[:, 1 + drow : array.shape[1] - 1 + drow, 1 + dcol : array.shape[2] - 1 + dcol]


def drive_with(field_ext, coeff_ext, rates, weights):
    center = neighbour(field_ext, 0, 0)
    coeff_mid = neighbour(coeff_ext, 0, 0)
    total = jnp.zeros_like(center)
    for drow, dcol in ((-1, 0), (1, 0), (0, -1), (0, 1)):
        total = total + (coeff_mid + neighbour(coeff_ext, drow, dcol)) * (
            neighbour(field_ext, drow, dcol) - center
        )
    total = total + rates[:, None, None] * (center - center * center * center)
    return (weights[:, None, None] * total).astype(jnp.bfloat16).reshape(center.shape[0], -1)


def rim_fields(field):
    return with_halo(field, (("gy", 1), ("gx", 2)), 1)


def body(modes_now, basis_rows, quad_weights, germ_nodes, log_fields, reaction_rates):
    k_local, rows_y, cols_x = modes_now.shape
    q_local, modes_total = basis_rows.shape
    log_ext = with_halo(log_fields, (("gy", 1), ("gx", 2)), 1)
    coeff_ext = jnp.exp(
        jnp.einsum("qj,jyx->qyx", germ_nodes, log_ext, precision=lax.Precision.HIGHEST)
    )

    def drive(field_ext):
        return drive_with(field_ext, coeff_ext, reaction_rates, quad_weights)

    current = modes_now.astype(jnp.float32)
    gathered = lax.all_gather(modes_now.reshape(k_local, -1), "quad", axis=0, tiled=True)
    field_zero = jnp.dot(basis_rows, gathered, preferred_element_type=jnp.float32)
    field_zero = rim_fields(field_zero.reshape(q_local, rows_y, cols_x))
    inner = gathered.reshape(modes_total, rows_y, cols_x)
    weighted_zero = drive(field_zero)
    partial_sum = lax.dot_general(
        basis_rows, weighted_zero, (((0,), (0,)), ((), ())), preferred_element_type=jnp.float32
    )
    summed = (
        lax.psum(partial_sum.astype(jnp.bfloat16), "quad")
        .astype(jnp.float32)
        .reshape(modes_total, rows_y, cols_x)
    )
    iterate_one = (inner.astype(jnp.float32) + time_step * summed).astype(jnp.bfloat16)
    flat = iterate_one.reshape(modes_total, -1)
    field_one = rim_fields(
        jnp.dot(basis_rows, flat, preferred_element_type=jnp.float32).reshape(
            q_local, rows_y, cols_x
        )
    )
    weighted = drive(field_one)
    second = (
        lax.psum_scatter(
            lax.dot_general(
                basis_rows, weighted, (((0,), (0,)), ((), ())), preferred_element_type=jnp.float32
            ).astype(jnp.bfloat16),
            "quad",
            scatter_dimension=0,
            tiled=True,
        )
        .astype(jnp.float32)
        .reshape(k_local, rows_y, cols_x)
    )
    return current + time_step * second


def solution(mesh):
    n, ny, nx = (mesh.shape[name] for name in ("quad", "gy", "gx"))
    planar = (ny, nx) == (2, 4) and n > 1
    run = functools.partial(fast_body, n, ny, nx) if planar else body
    in_specs = (
        P("quad", "gy", "gx"),
        P("quad", None),
        P("quad"),
        P("quad", None),
        P(None, "gy", "gx"),
        P("quad"),
    )
    out_specs = P("quad", "gy", "gx")
    return jax.shard_map(run, mesh=mesh, in_specs=in_specs, out_specs=out_specs, check_vma=False)
```
